128 devices in a mesh: group: 2 (over core), fsdp: 8 (over z, x_hi), tensor: 8 (over x_lo, y).
Axes of the slice: x: 4 (x_hi: 2, x_lo: 2; x = x_hi * 2 + x_lo), y: 4, z: 4, core: 2. Of those that a mesh axis runs over, the one named last changes fastest.
Arguments:
- master: float32 [8192, 6144], P('tensor', ('group', 'fsdp')), may hold values from -6 to 6
- moment: float32 [8192, 6144], P('tensor', ('group', 'fsdp')), may hold values from -4 to 4
- second: float32 [8192, 6144], P('tensor', ('group', 'fsdp')), may hold values from 0.001 to 0.2
- gradient: bfloat16 [8192, 6144], P('tensor', ('group', 'fsdp')), may hold values from -20000 to 20000
- prior_weights: bfloat16 [8192, 6144], P(None, 'tensor'), may hold values from -6 to 6
- tokens: bfloat16 [16, 1024, 8192], P(('group', 'fsdp'), None, 'tensor'), may hold values from -5000 to 5000
- norm_gain: float32 [8192], replicated, may hold values from 0.6 to 24
- segment_ids: int32 [16, 1024], P(('group', 'fsdp')), may hold values from 0 to 3, never falling along the last dimension, each value on 1 to 512 neighbouring positions
Outputs:
- new_master: float32 [8192, 6144], P('tensor', ('group', 'fsdp'))
- new_moment: float32 [8192, 6144], P('tensor', ('group', 'fsdp'))
- new_second: float32 [8192, 6144], P('tensor', ('group', 'fsdp'))
- attended: bfloat16 [16, 1024, 4096], P(('group', 'fsdp'), None, 'tensor')
The draws below stay inside these ranges and needn't reach their ends.
Inputs may be any that keep to these rules, and one draw needn't show every extreme that they name: `segment_ids`: ids never fall along a row; a document holds at most half of a row's tokens.
All inputs are finite; a program needn't handle non-finite values.
Results may differ from the reference program's by a relative error of at most 0.04.
The reference program's roundings to bfloat16 on the way count: a program that leaves them out, or rounds other values in their place, can miss the bound.
Values may be sent and summed in bfloat16 or wider, within the bound.
A program may use at most 192 MiB of HBM per device.

```python
import math
import jax
import jax.numpy as jnp
import numpy as np
from jax import lax

D = 8192
HD = 128
KVH = 8
QPK = 4
TOK_DEV = 1024
QKV = 6144
ROWS = 16


def draw_gradient(key, part):
    key = jax.random.fold_in(key, 11)
    noise_key, row_key, col_key = jax.random.split(key, 3)
    row_ramp = 3.0 ** (0.5 * jnp.arange(D).astype(jnp.float32) / D)
    col_ramp = 3.0 ** (0.5 * jnp.arange(QKV).astype(jnp.float32) / QKV)
    row_scale = 10.0 ** jax.random.uniform(row_key, (D,)) * row_ramp
    col_scale = 10.0 ** jax.random.uniform(col_key, (QKV,)) * col_ramp
    base = jnp.clip(jax.random.normal(noise_key, (D, QKV)), -4.0, 4.0)
    return (base * row_scale[:, None] * col_scale[None, :]).astype(jnp.bfloat16)


def draw_tokens(key, part):
    key = jax.random.fold_in(key, 23)
    noise_key, row_key, feature_key = jax.random.split(key, 3)
    row_scale = 10.0 ** jax.random.uniform(row_key, (ROWS, TOK_DEV, 1))
    feature_scale = 10.0 ** jax.random.uniform(feature_key, (D,)) * 3.0 ** (0.5 * jnp.arange(D).astype(jnp.float32) / D)
    base = jnp.clip(jax.random.normal(noise_key, (ROWS, TOK_DEV, D)), -4.0, 4.0)
    return (base * row_scale * feature_scale[None, None, :]).astype(jnp.bfloat16)


def draw_norm_gain(key, part):
    key = jax.random.fold_in(key, 37)
    return jax.random.uniform(key, (D,), minval=0.6, maxval=1.6).astype(jnp.float32)


def level_of(stream_key, dims, pieces, low, top_value):
    gain = 1.0
    for dim, shards_of in pieces:
        draws = jax.random.uniform(jax.random.fold_in(jax.random.fold_in(stream_key, 6), dim), (shards_of,), jnp.float32, low / len(pieces), top_value / len(pieces))
        gain = gain * jnp.repeat(jnp.exp(draws), dims[dim] // shards_of).reshape((-1,) + (1,) * (len(dims) - 1 - dim))
    return gain


def profile(number_of, total, bound, slope):
    portions = [(1 << 20) // math.isqrt(standing ** slope) + 1 for standing in range(2, number_of + 1)]
    spare, holding = total - bound - (number_of - 1), [1] * (number_of - 1)
    while spare > 0:
        movable = [i for i in range(number_of - 1) if holding[i] < bound]
        whole, left = sum([portions[i] for i in movable]), spare
        for i in movable:
            addition = min(bound - holding[i], max(1, left * portions[i] // whole), spare)
            holding[i] = holding[i] + addition
            spare = spare - addition
    return np.array([bound] + holding)


def uneven_parts(key, number_of, total, limit, skew):
    if number_of == 2:
        one = jax.random.randint(key, (), max(1, total - limit), min(limit, total - 1) + 1)
        return jnp.stack([one, total - one])
    sizes = jnp.asarray(profile(number_of, total, limit, skew), jnp.int32)
    twos = (number_of - 1) // 2
    source_of, receiver = sizes[1:1 + 2 * twos:2], sizes[2:2 + 2 * twos:2]
    room = jnp.minimum(source_of - 1, limit - receiver)
    shifted = jax.random.randint(jax.random.fold_in(key, 1), (twos,), 0, 1 << 20) % (room + 1)
    sizes = sizes.at[1:1 + 2 * twos:2].set(source_of - shifted).at[2:2 + 2 * twos:2].set(receiver + shifted)
    return sizes[jax.random.permutation(jax.random.fold_in(key, 2), number_of)]


def gaussian(stream_key, shape, deviation, limit, shards=(), dtype=jnp.bfloat16):
    array = jax.random.normal(stream_key, shape, jnp.float32) * deviation
    if len(shards) > 0:
        array = level_of(stream_key, shape, shards, -0.22, 0.18) * array
    return jnp.clip(array, min=-limit, max=limit).astype(dtype)


def setup_inputs(seed: int = 0) -> dict:
    splits = jax.random.split(jax.random.key(seed), 9)
    return {
        "master": gaussian(splits[0], (D, QKV), 1.0, 6.0, ((0, 8), (1, 16)), jnp.float32),
        "moment": gaussian(splits[1], (D, QKV), 0.3, 4.0, ((0, 8), (1, 16)), jnp.float32),
        "second": jnp.clip(jnp.exp(math.log(0.2) - 5.2983173 * jax.random.uniform(splits[2], (D, QKV), jnp.float32) ** level_of(splits[2], (D, QKV), ((0, 8), (1, 16)), -0.2, 0.2)), 0.001, 0.2),
        "gradient": draw_gradient(jax.random.fold_in(splits[8], 71), 0),
        "prior_weights": gaussian(splits[4], (D, QKV), 1.0, 6.0, ((1, 8),)),
        "tokens": draw_tokens(jax.random.fold_in(splits[8], 71), 0),
        "norm_gain": draw_norm_gain(jax.random.fold_in(splits[8], 71), 0),
        "segment_ids": jax.vmap(lambda own: jnp.searchsorted(jnp.cumsum(uneven_parts(own, 4, TOK_DEV, TOK_DEV // 2, 0)), jnp.arange(TOK_DEV), side="right"))(jax.random.split(splits[7], ROWS)).reshape((ROWS, TOK_DEV)).astype(jnp.int32),
    }


learn_rate = 0.01
decay_rate = 0.1
clip_rms = 0.25
first_fix = 1.0 - math.exp(200.0 * math.log(0.9))
second_fix = 1.0 - math.exp(200.0 * math.log(0.95))
mix_share = 0.6

def rotary(values, token_count):
    head_width = values.shape[-1]
    half_width = head_width // 2
    places = jnp.arange(token_count).astype(jnp.float32)
    frequencies = 500000.0 ** (-(jnp.arange(half_width).astype(jnp.float32) * 2.0 / head_width))
    angles = places[:, None] * frequencies[None, :]
    cosine = jnp.cos(angles)[:, None, :]
    sine_table = jnp.sin(angles)[:, None, :]
    front_half = values[..., :half_width]
    back_half = values[..., half_width:]
    return jnp.concatenate([front_half * cosine - back_half * sine_table, back_half * cosine + front_half * sine_table], axis=-1)

def attend(projected, segments):
    token_count = projected.shape[0]
    groups = projected.shape[1]
    queries = rotary(projected[:, :, :QPK, :].reshape(token_count, groups * QPK, HD), token_count)
    queries = queries.astype(jnp.bfloat16).reshape(token_count, groups, QPK, HD)
    keys = rotary(projected[:, :, QPK, :], token_count).astype(jnp.bfloat16)
    values = projected[:, :, QPK + 1, :].astype(jnp.bfloat16)
    scores = jnp.einsum('qgph,kgh->gpqk', queries.astype(jnp.float32), keys.astype(jnp.float32)) * HD ** (-0.5)
    places = jnp.arange(token_count)
    allowed = (segments[:, None] == segments[None, :]) & (places[:, None] >= places[None, :])
    scores = jnp.where(allowed[None, None], scores, -jnp.inf)
    row_top = lax.optimization_barrier(jnp.max(scores, axis=-1, keepdims=True))
    weights = jnp.exp(scores - row_top)
    weights_half = (weights / lax.optimization_barrier(jnp.sum(weights, axis=-1, keepdims=True))).astype(jnp.bfloat16)
    output = jnp.einsum('gpqk,kgh->qgph', weights_half.astype(jnp.float32), values.astype(jnp.float32))
    return output.reshape(token_count, groups * QPK * HD).astype(jnp.bfloat16)

def reference(master, moment, second, gradient, prior_weights, tokens, norm_gain, segment_ids):
    grad_values = gradient.astype(jnp.float32)
    overall = jnp.sum(grad_values * grad_values)
    clip_factor = jnp.minimum(1.0, clip_rms * math.sqrt(D * QKV) / (jnp.sqrt(overall) + 1e-06))
    clipped = clip_factor * grad_values
    new_moment = 0.9 * moment + 0.1 * clipped
    new_second = 0.95 * second + 0.05 * clipped * clipped
    update = new_moment / first_fix / (jnp.sqrt(new_second / second_fix) + 1e-08) + decay_rate * master
    new_master = master - learn_rate * update
    policy_half = new_master.astype(jnp.bfloat16)
    mixed_panel = (mix_share * policy_half.astype(jnp.float32) + (1.0 - mix_share) * prior_weights.astype(jnp.float32)).astype(jnp.bfloat16)
    mixed_wide = mixed_panel.astype(jnp.float32)

    def one_row(inputs):
        row_tokens, segments = inputs
        values = row_tokens.astype(jnp.float32)
        inverse = lax.rsqrt(lax.optimization_barrier(jnp.sum(values * values, axis=1)) / D + 1e-05)
        normed = (values * inverse[:, None] * norm_gain[None, :]).astype(jnp.bfloat16)
        projected = jnp.dot(normed.astype(jnp.float32), mixed_wide, precision=lax.Precision.HIGHEST) * D ** (-0.5)
        return attend(projected.reshape(TOK_DEV, KVH, QPK + 2, HD), segments)
    attended = lax.map(one_row, (tokens, segment_ids))
    return (new_master, new_moment, new_second, attended)
```

```python
import functools
import math

import jax
import jax.numpy as jnp
import numpy as np
from jax import lax
from jax.experimental import pallas as pl
from jax.experimental.pallas import tpu as pltpu
from jax.sharding import PartitionSpec as P

D = 8192
HD = 128
QPK = 4
QKV = 6144

learn_rate = 0.01
decay_rate = 0.1
clip_rms = 0.25
first_fix = 1.0 - math.exp(200.0 * math.log(0.9))
second_fix = 1.0 - math.exp(200.0 * math.log(0.95))
mix_share = 0.6

MESH = pl.DeviceIdType.MESH
F32 = jnp.float32
BF16 = jnp.bfloat16
SUM_TYPE = BF16
TOK = 1024
FEAT = 1024
COLS = 384
PIECES = 4
PIECE = TOK // PIECES
ORDER = (2, 1, 0)


def rotary_tables():
    places = np.arange(TOK).astype(np.float32)
    lanes = np.arange(HD // 2).astype(np.float32)
    frequencies = np.power(500000.0, -(lanes * np.float32(2.0) / np.float32(HD)).astype(np.float64))
    angles = places[:, None] * frequencies.astype(np.float32)[None, :]
    cosine = np.cos(angles.astype(np.float64)).astype(np.float32)
    sine = np.sin(angles.astype(np.float64)).astype(np.float32)
    return np.stack(
        [np.concatenate([cosine, cosine], 1), np.concatenate([-sine, sine], 1)]
    ).astype(np.float32)


def adam(master, moment, second, grad, clip):
    clipped = clip * grad
    new_moment = 0.9 * moment + 0.1 * clipped
    new_second = 0.95 * second + 0.05 * clipped * clipped
    update = (
        new_moment / first_fix / (jnp.sqrt(new_second / second_fix) + 1e-08) + decay_rate * master
    )
    return master - learn_rate * update, new_moment, new_second


def push(src, dst, send, recv, where):
    return pltpu.make_async_remote_copy(
        src_ref=src, dst_ref=dst, send_sem=send, recv_sem=recv, device_id=where, device_id_type=MESH
    )


def project_kernel(
    master_ref, moment_ref, second_ref, grad_ref, prior_ref, tok_ref, gain_ref, table_ref,
    qkv_ref, clip_ref,
    raw, normed, w, mas, mom, sec, gra, inv, msg_a, msg_b, s1_out, s1_in, pri, own, ps_out, ps_in,
    load_sem, tok_s, tok_r, fwd_s, fwd_r, a_s, a_r, b_s, b_r, pri_s, pri_r, s1_s, s1_r, hx_s, hx_r,
    z_s, z_r, zf_s, zf_r, sib_s, sib_r, ps_s, ps_r,
):
    g = lax.axis_index("group")
    f = lax.axis_index("fsdp")
    t = lax.axis_index("tensor")
    z, h = f // 2, f % 2
    l, y = t // 4, t % 4
    y_up, y_down, y_far = (y + 1) % 4, (y + 3) % 4, (y + 2) % 4
    z_up, z_down, z_far = (z + 1) % 4, (z + 3) % 4, (z + 2) % 4
    at_y_up, at_y_down = (g, f, l * 4 + y_up), (g, f, l * 4 + y_down)
    at_z_up, at_z_down = (g, z_up * 2 + h, t), (g, z_down * 2 + h, t)
    at_x = (g, f, (1 - l) * 4 + y)
    at_h = (g, z * 2 + (1 - h), t)
    at_core = (1 - g, f, t)
    at_swap = (g, y * 2 + h, l * 4 + z)
    straight = y == z
    mine = g * 8 + f

    loads = [
        pltpu.make_async_copy(grad_ref, gra, load_sem.at[0]),
        pltpu.make_async_copy(tok_ref, raw.at[y], load_sem.at[1]),
        pltpu.make_async_copy(master_ref, mas, load_sem.at[2]),
        pltpu.make_async_copy(moment_ref, mom, load_sem.at[3]),
        pltpu.make_async_copy(second_ref, sec, load_sem.at[4]),
    ]
    for load in loads:
        load.start()
    prior_cols = pl.ds(pl.multiple_of(h * COLS, 128), COLS)
    prior_here = pltpu.make_async_copy(
        prior_ref.at[pl.ds(pl.multiple_of((l * 4 + z) * FEAT, FEAT), FEAT), prior_cols], pri, load_sem.at[5]
    )
    prior_push = push(
        prior_ref.at[pl.ds(pl.multiple_of(((1 - l) * 4 + z) * FEAT, FEAT), FEAT), prior_cols],
        pri, pri_s, pri_r, at_x,
    )
    holds_prior = g == l

    peers_a = [(g, f, (t + d) % 8) for d in range(1, 8)]
    places_b = [(mine + d) % 16 for d in range(1, 16)]
    peers_b = [(place // 8, place % 8, t) for place in places_b]

    barrier = pltpu.get_barrier_semaphore()
    for peer in peers_a + peers_b:
        pl.semaphore_signal(barrier, inc=1, device_id=peer, device_id_type=MESH)

    @pl.when(jnp.logical_not(straight))
    def _():
        pl.semaphore_signal(barrier, inc=1, device_id=at_swap, device_id_type=MESH)
        pl.semaphore_wait(barrier, 23)

    @pl.when(straight)
    def _():
        pl.semaphore_wait(barrier, 22)

    tok_pushes = []
    for p in range(PIECES):
        rows = pl.ds(p * PIECE, PIECE)
        for way, where in ((0, at_y_up), (1, at_y_down)):
            copy = push(tok_ref.at[rows, :], raw.at[y, rows, :], tok_s.at[way, p], tok_r.at[way, p], where)
            copy.start()
            tok_pushes.append(copy)

    @pl.when(holds_prior)
    def _():
        prior_push.start()
        prior_here.start()

    loads[0].wait()

    def grad_sum(i, total):
        v = gra[pl.ds(pl.multiple_of(i * 64, 64), 64), :].astype(F32)
        return total + jnp.sum((v * v).reshape(8, 8, COLS), axis=0)

    total = lax.fori_loop(0, FEAT // 64, grad_sum, jnp.zeros((8, COLS), F32))
    msg_a[t, 8:16, :] = total[:, 0:128] + total[:, 128:256] + total[:, 256:384]
    loads[1].wait()
    for i in range(8):
        part = jnp.zeros((128, 128), F32)
        for j in range(FEAT // 128):
            v = raw[y, i * 128:(i + 1) * 128, j * 128:(j + 1) * 128].astype(F32)
            part = part + v * v
        msg_a[t, i:i + 1, :] = jnp.sum(part.T, axis=0, keepdims=True)
    a_pushes = [
        push(msg_a.at[t], msg_a.at[t], a_s.at[d], a_r.at[d], peer) for d, peer in enumerate(peers_a)
    ]
    for copy in a_pushes:
        copy.start()
    for d in range(7):
        source = (t + 7 - d) % 8
        push(msg_a.at[source], msg_a.at[source], a_s.at[d], a_r.at[d], peers_a[d]).wait_recv()
    sums = msg_a[0]
    for s in range(1, 8):
        sums = sums + msg_a[s]
    msg_b[mine] = sums[8:16, :]
    b_pushes = [
        push(msg_b.at[mine], msg_b.at[mine], b_s.at[d], b_r.at[d], peer) for d, peer in enumerate(peers_b)
    ]
    for copy in b_pushes:
        copy.start()
    inverse = lax.rsqrt(sums[0:8, :] / D + 1e-05)
    for i in range(8):
        inv[i * 128:(i + 1) * 128, :] = jnp.broadcast_to(inverse[i:i + 1, :], (128, 128)).T
    for d in range(15):
        source = (mine + 15 - d) % 16
        push(msg_b.at[source], msg_b.at[source], b_s.at[d], b_r.at[d], peers_b[d]).wait_recv()
    sums = msg_b[0]
    for s in range(1, 16):
        sums = sums + msg_b[s]
    overall = jnp.broadcast_to(jnp.sum(sums, keepdims=True), (8, 128))
    clip_ref[...] = jnp.minimum(1.0, clip_rms * math.sqrt(D * QKV) / (jnp.sqrt(overall) + 1e-06))

    for load in loads[2:]:
        load.wait()
    s1_pushes, s1_copies = [None] * 3, [None] * 3
    for c in ORDER:
        cols = slice(c * 128, (c + 1) * 128)

        def step(i, carry, c=c, cols=cols):
            rows = pl.ds(pl.multiple_of(i * 64, 64), 64)
            updated, _, _ = adam(
                mas[rows, cols], mom[rows, cols], sec[rows, cols], gra[rows, cols].astype(F32), clip_ref[0:1, :]
            )
            s1_out[c, rows, :] = updated.astype(BF16)
            return carry

        lax.fori_loop(0, FEAT // 64, step, 0)
        s1_pushes[c] = push(s1_out.at[c], s1_in.at[c], s1_s.at[c], s1_r.at[c], at_swap)
        s1_copies[c] = pltpu.make_async_copy(s1_out.at[c], s1_in.at[c], s1_r.at[c])

        @pl.when(jnp.logical_not(straight))
        def _(c=c):
            s1_pushes[c].start()

        @pl.when(straight)
        def _(c=c):
            s1_copies[c].start()

    def normalize(block):
        gain = gain_ref[l * 4 + block]

        def step(i, carry):
            rows = pl.ds(pl.multiple_of(i * 64, 64), 64)
            scale = jnp.concatenate([inv[rows, :]] * (FEAT // 128), axis=1)
            normed[block, rows, :] = (raw[block, rows, :].astype(F32) * scale * gain).astype(BF16)
            return carry

        lax.fori_loop(0, TOK // 64, step, 0)

    normalize(y)

    @pl.when(holds_prior)
    def _():
        prior_here.wait()

    @pl.when(jnp.logical_not(holds_prior))
    def _():
        prior_push.wait_recv()

    here = pl.ds(pl.multiple_of(h * 128, 128), 128)
    hx_pushes = [None] * 3
    for c in ORDER:
        @pl.when(jnp.logical_not(straight))
        def _(c=c):
            s1_pushes[c].wait_recv()

        @pl.when(straight)
        def _(c=c):
            s1_copies[c].wait()

        def step(i, carry, c=c):
            rows = pl.ds(pl.multiple_of(i * 64, 64), 64)
            policy = s1_in[c, rows, :].astype(F32)
            prior = pri[rows, c * 128:(c + 1) * 128].astype(F32)
            w[c, z, g, rows, here] = (mix_share * policy + (1.0 - mix_share) * prior).astype(BF16)
            return carry

        lax.fori_loop(0, FEAT // 64, step, 0)
        block = w.at[c, z, g, :, here]
        hx_pushes[c] = push(block, block, hx_s.at[c], hx_r.at[c], at_h)
        hx_pushes[c].start()

    z_pushes, zf_pushes, sib_pushes = {}, {}, {}

    def share(c, slot, where):
        block = w.at[c, where, g]
        sib_pushes[c, slot] = push(block, block, sib_s.at[c, slot], sib_r.at[c, slot], at_core)
        sib_pushes[c, slot].start()

    there = pl.ds(pl.multiple_of((1 - h) * 128, 128), 128)
    for c in ORDER:
        came = w.at[c, z, g, :, there]
        push(came, came, hx_s.at[c], hx_r.at[c], at_h).wait_recv()
        block = w.at[c, z, g]
        for way, where in ((0, at_z_up), (1, at_z_down)):
            z_pushes[c, way] = push(block, block, z_s.at[c, way], z_r.at[c, way], where)
            z_pushes[c, way].start()
        share(c, 0, z)

    fwd_pushes = []
    half = PIECES // 2
    for p in range(half):
        for way, source, where, piece in ((0, y_down, at_y_up, p), (1, y_up, at_y_down, p + half)):
            block = raw.at[source, pl.ds(piece * PIECE, PIECE), :]
            push(block, block, tok_s.at[way, piece], tok_r.at[way, piece], where).wait_recv()
            copy = push(block, block, fwd_s.at[way, p], fwd_r.at[way, p], where)
            copy.start()
            fwd_pushes.append(copy)
    for p in range(half):
        for way, source, where, piece in ((0, y_down, at_y_up, p + half), (1, y_up, at_y_down, p)):
            block = raw.at[source, pl.ds(piece * PIECE, PIECE), :]
            push(block, block, tok_s.at[way, piece], tok_r.at[way, piece], where).wait_recv()
    normalize(y_down)
    normalize(y_up)

    for c in ORDER:
        for way, source, where in ((0, z_down, at_z_up), (1, z_up, at_z_down)):
            came = w.at[c, source, g]
            push(came, came, z_s.at[c, way], z_r.at[c, way], where).wait_recv()
            block = w.at[c, source, g, :, pl.ds(way * 128, 128)]
            zf_pushes[c, way] = push(block, block, zf_s.at[c, way], zf_r.at[c, way], where)
            zf_pushes[c, way].start()
            share(c, 1 + way, source)

    for p in range(half):
        for way, where, piece in ((0, at_y_up, p), (1, at_y_down, p + half)):
            block = raw.at[y_far, pl.ds(piece * PIECE, PIECE), :]
            push(block, block, fwd_s.at[way, p], fwd_r.at[way, p], where).wait_recv()
    normalize(y_far)

    def multiply(c, panel, out):
        def step(i, carry):
            rows = pl.ds(pl.multiple_of(i * 512, 512), 512)
            total = jnp.dot(normed[0, rows, :], w[c, 0, panel], preferred_element_type=F32)
            for block in range(1, 4):
                total = total + jnp.dot(normed[block, rows, :], w[c, block, panel], preferred_element_type=F32)
            out[c, rows, :] = total.astype(out.dtype)
            return carry

        lax.fori_loop(0, TOK // 512, step, 0)

    def finish(c):
        ps_pushes[c].wait_recv()

        def step(i, carry):
            rows = pl.ds(pl.multiple_of(i * 64, 64), 64)
            pair = (own[c, rows, :] + ps_in[c, rows, :].astype(F32)) * D ** (-0.5)
            for head, values in ((c, pair[:, 0:128]), (3 + c, pair[:, 128:256])):
                if head < 5:
                    turned = jnp.concatenate([values[:, 64:], values[:, :64]], axis=1)
                    values = values * table_ref[0, rows, :] + turned * table_ref[1, rows, :]
                qkv_ref[head, rows, :] = values.astype(BF16)
            return carry

        lax.fori_loop(0, TOK // 64, step, 0)

    ps_pushes = [None] * 3
    for place, c in enumerate(ORDER):
        for way, where in ((0, at_z_up), (1, at_z_down)):
            came = w.at[c, z_far, g, :, pl.ds(way * 128, 128)]
            push(came, came, zf_s.at[c, way], zf_r.at[c, way], where).wait_recv()
        share(c, 3, z_far)
        for slot, source in enumerate((z, z_down, z_up, z_far)):
            came = w.at[c, source, 1 - g]
            push(came, came, sib_s.at[c, slot], sib_r.at[c, slot], at_core).wait_recv()
        multiply(c, 1 - l, ps_out)
        ps_pushes[c] = push(ps_out.at[c], ps_in.at[c], ps_s.at[c], ps_r.at[c], at_x)
        ps_pushes[c].start()
        multiply(c, l, own)
        if place > 0:
            finish(ORDER[place - 1])
    finish(ORDER[-1])

    for copy in tok_pushes + fwd_pushes + a_pushes + b_pushes + hx_pushes + ps_pushes:
        copy.wait_send()
    for copies in (z_pushes, zf_pushes, sib_pushes):
        for copy in copies.values():
            copy.wait_send()

    @pl.when(holds_prior)
    def _():
        prior_push.wait_send()

    @pl.when(jnp.logical_not(straight))
    def _():
        for c in range(3):
            s1_pushes[c].wait_send()


def project(master, moment, second, gradient, prior, tokens, gain, tables):
    dma = pltpu.SemaphoreType.DMA
    vmem = pl.BlockSpec(memory_space=pltpu.VMEM)
    hbm = pl.BlockSpec(memory_space=pl.ANY)
    return pl.pallas_call(
        project_kernel,
        out_shape=(
            jax.ShapeDtypeStruct((QPK + 2, TOK, HD), BF16),
            jax.ShapeDtypeStruct((8, 128), F32),
        ),
        in_specs=[hbm] * 6 + [vmem] * 2,
        out_specs=(vmem, vmem),
        scratch_shapes=[
            pltpu.VMEM((4, TOK, FEAT), BF16),
            pltpu.VMEM((4, TOK, FEAT), BF16),
            pltpu.VMEM((3, 4, 2, FEAT, 256), BF16),
            pltpu.VMEM((FEAT, COLS), F32),
            pltpu.VMEM((FEAT, COLS), F32),
            pltpu.VMEM((FEAT, COLS), F32),
            pltpu.VMEM((FEAT, COLS), BF16),
            pltpu.VMEM((TOK, 128), F32),
            pltpu.VMEM((8, 16, 128), F32),
            pltpu.VMEM((16, 8, 128), F32),
            pltpu.VMEM((3, FEAT, 128), BF16),
            pltpu.VMEM((3, FEAT, 128), BF16),
            pltpu.VMEM((FEAT, COLS), BF16),
            pltpu.VMEM((3, TOK, 256), F32),
            pltpu.VMEM((3, TOK, 256), SUM_TYPE),
            pltpu.VMEM((3, TOK, 256), SUM_TYPE),
            dma((6,)),
            dma((2, PIECES)), dma((2, PIECES)), dma((2, PIECES // 2)), dma((2, PIECES // 2)),
            dma((7,)), dma((7,)), dma((15,)), dma((15,)),
            dma, dma, dma((3,)), dma((3,)), dma((3,)), dma((3,)),
            dma((3, 2)), dma((3, 2)), dma((3, 2)), dma((3, 2)),
            dma((3, 4)), dma((3, 4)), dma((3,)), dma((3,)),
        ],
        compiler_params=pltpu.CompilerParams(
            collective_id=0, has_side_effects=True, vmem_limit_bytes=60 * 1024 * 1024
        ),
        cost_estimate=pl.CostEstimate(
            flops=2 * TOK * D * 768, bytes_accessed=24 * 1024 * 1024, transcendentals=0
        ),
    )(master, moment, second, gradient, prior, tokens, gain, tables)


BLOCK = 256


def attend_kernel(
    qkv_ref, clip_ref, seg_ref, master_ref, moment_ref, second_ref, grad_ref,
    new_master_ref, new_moment_ref, new_second_ref, out_ref,
):
    place = pl.program_id(0)

    def adam_rows(i, carry):
        rows = pl.ds(pl.multiple_of(i * 32, 32), 32)
        clip = jnp.concatenate([clip_ref[0:1, :]] * 3, axis=1)
        new_master, new_moment, new_second = adam(
            master_ref[rows, :], moment_ref[rows, :], second_ref[rows, :], grad_ref[rows, :].astype(F32), clip
        )
        new_master_ref[rows, :] = new_master
        new_moment_ref[rows, :] = new_moment
        new_second_ref[rows, :] = new_second
        return carry

    lax.fori_loop(0, BLOCK // 32, adam_rows, 0)

    for q in range(TOK // BLOCK):
        @pl.when(place == q)
        def _(q=q):
            first = max(0, q - 2) * BLOCK
            last = (q + 1) * BLOCK
            width = last - first
            segments = seg_ref[0:1, :].astype(F32)
            column = jnp.concatenate(
                [
                    jnp.broadcast_to(segments[:, s:s + 128], (128, 128)).T
                    for s in range(q * BLOCK, last, 128)
                ],
                axis=0,
            )
            same = jnp.concatenate([column] * (width // 128), axis=1) == segments[:, first:last]
            at_query = lax.broadcasted_iota(jnp.int32, (BLOCK, width), 0) + q * BLOCK
            at_key = lax.broadcasted_iota(jnp.int32, (BLOCK, width), 1) + first
            allowed = same & (at_query >= at_key)
            for head in range(QPK):
                scores = lax.dot_general(
                    qkv_ref[head, q * BLOCK:last, :], qkv_ref[QPK, first:last, :],
                    (((1,), (1,)), ((), ())), preferred_element_type=F32,
                ) * HD ** (-0.5)
                scores = jnp.where(allowed, scores, -jnp.inf)
                weights = jnp.exp(scores - jnp.max(scores, axis=1, keepdims=True))
                weights = (weights / jnp.sum(weights, axis=1, keepdims=True)).astype(BF16)
                out_ref[:, head * HD:(head + 1) * HD] = jnp.dot(
                    weights, qkv_ref[QPK + 1, first:last, :], preferred_element_type=F32
                ).astype(BF16)


def attend(qkv, clip, segments, master, moment, second, gradient):
    steps = TOK // BLOCK
    rows = pl.BlockSpec((BLOCK, COLS), lambda i: (i, 0))
    return pl.pallas_call(
        attend_kernel,
        grid=(steps,),
        out_shape=(
            jax.ShapeDtypeStruct((FEAT, COLS), F32),
            jax.ShapeDtypeStruct((FEAT, COLS), F32),
            jax.ShapeDtypeStruct((FEAT, COLS), F32),
            jax.ShapeDtypeStruct((TOK, QPK * HD), BF16),
        ),
        in_specs=[
            pl.BlockSpec((QPK + 2, TOK, HD), lambda i: (0, 0, 0)),
            pl.BlockSpec((8, 128), lambda i: (0, 0)),
            pl.BlockSpec((1, TOK), lambda i: (0, 0)),
            rows, rows, rows, rows,
        ],
        out_specs=(rows, rows, rows, pl.BlockSpec((BLOCK, QPK * HD), lambda i: (i, 0))),
        compiler_params=pltpu.CompilerParams(vmem_limit_bytes=48 * 1024 * 1024),
    )(qkv, clip, segments, master, moment, second, gradient)


def shards(master, moment, second, gradient, prior_weights, tokens, norm_gain, segment_ids):
    qkv, clip = project(
        master, moment, second, gradient, prior_weights, tokens[0], norm_gain.reshape(8, 1, FEAT),
        jnp.asarray(rotary_tables()),
    )
    new_master, new_moment, new_second, attended = attend(
        qkv, clip, segment_ids, master, moment, second, gradient
    )
    return (new_master, new_moment, new_second, attended[None])


def solution(mesh):
    in_specs = (
        P("tensor", ("group", "fsdp")),
        P("tensor", ("group", "fsdp")),
        P("tensor", ("group", "fsdp")),
        P("tensor", ("group", "fsdp")),
        P(None, "tensor"),
        P(("group", "fsdp"), None, "tensor"),
        P(),
        P(("group", "fsdp"), None),
    )
    out_specs = (
        P("tensor", ("group", "fsdp")),
        P("tensor", ("group", "fsdp")),
        P("tensor", ("group", "fsdp")),
        P(("group", "fsdp"), None, "tensor"),
    )
    return jax.shard_map(shards, mesh=mesh, in_specs=in_specs, out_specs=out_specs, check_vma=False)
```

```python
import functools
import math

import jax
import jax.numpy as jnp
import numpy as np
from jax import lax
from jax.experimental import pallas as pl
from jax.experimental.pallas import tpu as pltpu
from jax.sharding import PartitionSpec as P

D = 8192
HD = 128
QPK = 4
QKV = 6144

learn_rate = 0.01
decay_rate = 0.1
clip_rms = 0.25
first_fix = 1.0 - math.exp(200.0 * math.log(0.9))
second_fix = 1.0 - math.exp(200.0 * math.log(0.95))
mix_share = 0.6

MESH = pl.DeviceIdType.MESH
F32 = jnp.float32
BF16 = jnp.bfloat16
SUM_TYPE = BF16
TOK = 1024
FEAT = 1024
COLS = 384
PIECES = 8
PIECE = TOK // PIECES
ORDER = (2, 1, 0)


def rotary_tables():
    places = np.arange(TOK).astype(np.float32)
    lanes = np.arange(HD // 2).astype(np.float32)
    frequencies = np.power(500000.0, -(lanes * np.float32(2.0) / np.float32(HD)).astype(np.float64))
    angles = places[:, None] * frequencies.astype(np.float32)[None, :]
    cosine = np.cos(angles.astype(np.float64)).astype(np.float32)
    sine = np.sin(angles.astype(np.float64)).astype(np.float32)
    return np.stack(
        [np.concatenate([cosine, cosine], 1), np.concatenate([-sine, sine], 1)]
    ).astype(np.float32)


def adam(master, moment, second, grad, clip):
    clipped = clip * grad
    new_moment = 0.9 * moment + 0.1 * clipped
    new_second = 0.95 * second + 0.05 * clipped * clipped
    update = (
        new_moment / first_fix / (jnp.sqrt(new_second / second_fix) + 1e-08) + decay_rate * master
    )
    return master - learn_rate * update, new_moment, new_second


def push(src, dst, send, recv, where):
    return pltpu.make_async_remote_copy(
        src_ref=src, dst_ref=dst, send_sem=send, recv_sem=recv, device_id=where, device_id_type=MESH
    )


def project_kernel(
    master_ref, moment_ref, second_ref, grad_ref, prior_ref, tok_ref, gain_ref, table_ref,
    qkv_ref, clip_ref,
    raw, normed, w, mas, mom, sec, gra, inv, msg_a, msg_b, msg_r, z_out, z_in, y_in, pri, own, ps_out, ps_in,
    load_sem, tok_s, tok_r, fwd_s, fwd_r, a_s, a_r, b_s, b_r, r_s, r_r, pri_s, pri_r,
    za_s, za_r, ya_s, ya_r, hx_s, hx_r, zg_s, zg_r, zf_s, zf_r, sib_s, sib_r, ps_s, ps_r,
):
    g = lax.axis_index("group")
    f = lax.axis_index("fsdp")
    t = lax.axis_index("tensor")
    z, h = f // 2, f % 2
    l, y = t // 4, t % 4
    y_up, y_down, y_far = (y + 1) % 4, (y + 3) % 4, (y + 2) % 4
    z_up, z_down, z_far = (z + 1) % 4, (z + 3) % 4, (z + 2) % 4
    at_y_up, at_y_down = (g, f, l * 4 + y_up), (g, f, l * 4 + y_down)
    at_z_up, at_z_down = (g, z_up * 2 + h, t), (g, z_down * 2 + h, t)
    at_x = (g, f, (1 - l) * 4 + y)
    at_h = (g, z * 2 + (1 - h), t)
    at_core = (1 - g, f, t)
    mine = g * 8 + f
    quarter = (z + 4 - y) % 4
    quarter_up, quarter_down, quarter_far = (quarter + 1) % 4, (quarter + 3) % 4, (quarter + 2) % 4

    loads = [
        pltpu.make_async_copy(grad_ref, gra, load_sem.at[0]),
        pltpu.make_async_copy(tok_ref, raw.at[y], load_sem.at[1]),
        pltpu.make_async_copy(master_ref, mas, load_sem.at[2]),
        pltpu.make_async_copy(moment_ref, mom, load_sem.at[3]),
        pltpu.make_async_copy(second_ref, sec, load_sem.at[4]),
    ]
    for load in loads:
        load.start()
    prior_cols = pl.ds(pl.multiple_of(h * COLS, 128), COLS)
    prior_here = pltpu.make_async_copy(
        prior_ref.at[pl.ds(l * 4, 4), quarter, :, prior_cols], pri, load_sem.at[5]
    )
    prior_push = push(
        prior_ref.at[pl.ds((1 - l) * 4, 4), quarter, :, prior_cols], pri, pri_s, pri_r, at_x
    )
    holds_prior = g == l

    peers_a = [(g, f, (t + d) % 8) for d in range(1, 8)]
    places_b = [(mine + d) % 16 for d in range(1, 16)]
    peers_b = [(place // 8, place % 8, t) for place in places_b]

    barrier = pltpu.get_barrier_semaphore()
    for peer in peers_a + peers_b:
        pl.semaphore_signal(barrier, inc=1, device_id=peer, device_id_type=MESH)

    loads[0].wait()

    def grad_sum(i, total):
        v = gra[pl.ds(pl.multiple_of(i * 64, 64), 64), :].astype(F32)
        return total + jnp.sum((v * v).reshape(8, 8, COLS), axis=0)

    total = lax.fori_loop(0, FEAT // 64, grad_sum, jnp.zeros((8, COLS), F32))
    msg_a[t] = total[:, 0:128] + total[:, 128:256] + total[:, 256:384]
    pl.semaphore_wait(barrier, 22)

    def send_all(msg, slot, send, recv, peers):
        copies = [push(msg.at[slot], msg.at[slot], send.at[d], recv.at[d], peer) for d, peer in enumerate(peers)]
        for copy in copies:
            copy.start()
        return copies

    def wait_all(msg, slot, send, recv, peers):
        count = len(peers) + 1
        for d, peer in enumerate(peers):
            source = (slot + count - 1 - d) % count
            push(msg.at[source], msg.at[source], send.at[d], recv.at[d], peer).wait_recv()
        sums = msg[0]
        for s in range(1, count):
            sums = sums + msg[s]
        return sums

    a_pushes = send_all(msg_a, t, a_s, a_r, peers_a)

    tok_pushes = []

    def tok_rows(piece):
        return pl.ds(piece * PIECE, PIECE)

    def own_pair(j):
        for piece in (2 * j, 2 * j + 1):
            for way, where in ((0, at_y_up), (1, at_y_down)):
                copy = push(
                    tok_ref.at[tok_rows(piece), :], raw.at[y, tok_rows(piece), :],
                    tok_s.at[way, piece], tok_r.at[way, piece], where,
                )
                copy.start()
                tok_pushes.append(copy)

    def forward_pair(j):
        for way, source, where in ((0, y_down, at_y_up), (1, y_up, at_y_down)):
            piece = 2 * j + way
            block = raw.at[source, tok_rows(piece), :]
            push(block, block, tok_s.at[way, piece], tok_r.at[way, piece], where).wait_recv()
            copy = push(block, block, fwd_s.at[way, j], fwd_r.at[way, j], where)
            copy.start()
            tok_pushes.append(copy)

    def normalize(block, j):
        gain = gain_ref[l * 4 + block]
        cols = pl.ds(pl.multiple_of(block * FEAT, FEAT), FEAT)

        def step(i, carry):
            rows = pl.ds(pl.multiple_of(j * 256 + i * 32, 32), 32)
            scale = jnp.concatenate([inv[rows, :]] * (FEAT // 128), axis=1)
            normed[rows, cols] = (raw[block, rows, :].astype(F32) * scale * gain).astype(BF16)
            return carry

        lax.fori_loop(0, 8, step, 0)

    def ready_pair(j):
        for way, source, where in ((0, y_down, at_y_up), (1, y_up, at_y_down)):
            piece = 2 * j + 1 - way
            block = raw.at[source, tok_rows(piece), :]
            push(block, block, tok_s.at[way, piece], tok_r.at[way, piece], where).wait_recv()
        normalize(y_down, j)
        normalize(y_up, j)
        for way, where in ((0, at_y_up), (1, at_y_down)):
            block = raw.at[y_far, tok_rows(2 * j + way), :]
            push(block, block, fwd_s.at[way, j], fwd_r.at[way, j], where).wait_recv()
        normalize(y_far, j)

    own_pair(0)

    @pl.when(holds_prior)
    def _():
        prior_push.start()
        prior_here.start()

    loads[1].wait()
    for i in range(8):
        part = jnp.zeros((128, 128), F32)
        for j in range(FEAT // 128):
            v = raw[y, i * 128:(i + 1) * 128, j * 128:(j + 1) * 128].astype(F32)
            part = part + v * v
        msg_r[t, i:i + 1, :] = jnp.sum(part.T, axis=0, keepdims=True)

    msg_b[mine] = wait_all(msg_a, t, a_s, a_r, peers_a)
    b_pushes = send_all(msg_b, mine, b_s, b_r, peers_b)
    r_pushes = send_all(msg_r, t, r_s, r_r, peers_a)
    sums = wait_all(msg_b, mine, b_s, b_r, peers_b)
    overall = jnp.broadcast_to(jnp.sum(sums, keepdims=True), (8, 128))
    clip_ref[...] = jnp.minimum(1.0, clip_rms * math.sqrt(D * QKV) / (jnp.sqrt(overall) + 1e-06))

    for load in loads[2:]:
        load.wait()
    za_pushes, ya_pushes, hx_pushes, zg_pushes, zf_pushes, sib_pushes, ps_pushes = {}, {}, {}, {}, {}, {}, {}

    def update(c):
        cols = slice(c * 128, (c + 1) * 128)

        def step(i, carry):
            rows = pl.ds(pl.multiple_of(i * 64, 64), 64)
            updated, _, _ = adam(
                mas[rows, cols], mom[rows, cols], sec[rows, cols], gra[rows, cols].astype(F32), clip_ref[0:1, :]
            )
            z_out[c, i // 4, pl.ds(pl.multiple_of(i % 4 * 64, 64), 64), :] = updated.astype(BF16)
            return carry

        lax.fori_loop(0, FEAT // 64, step, 0)
        for d in range(1, 4):
            za_pushes[c, d] = push(
                z_out.at[c, d], z_in.at[c, d], za_s.at[c, d - 1], za_r.at[c, d - 1], (g, (z + d) % 4 * 2 + h, t)
            )
            za_pushes[c, d].start()
        z_in[c, 0] = z_out[c, 0]

    def deal(c):
        for d in range(1, 4):
            za_pushes[c, d].wait_recv()
        for d in range(1, 4):
            other = (y + d) % 4
            ya_pushes[c, d] = push(
                z_in.at[c, (z + 4 - other) % 4], y_in.at[c, y], ya_s.at[c, d - 1], ya_r.at[c, d - 1],
                (g, f, l * 4 + other),
            )
            ya_pushes[c, d].start()
        y_in[c, y] = z_in[c, quarter]

    here = pl.ds(pl.multiple_of(h * 128, 128), 128)
    there = pl.ds(pl.multiple_of((1 - h) * 128, 128), 128)

    def part_of(c, q, cols):
        return w.at[c, :, g, q, :, cols]

    def mix(c):
        for d in range(1, 4):
            block = y_in.at[c, (y + 4 - d) % 4]
            push(block, block, ya_s.at[c, d - 1], ya_r.at[c, d - 1], (g, f, l * 4 + (y + d) % 4)).wait_recv()
        for block in range(4):
            policy = y_in[c, block].astype(F32)
            prior = pri[block, :, c * 128:(c + 1) * 128].astype(F32)
            w[c, block, g, quarter, :, here] = (mix_share * policy + (1.0 - mix_share) * prior).astype(BF16)
        block = part_of(c, quarter, here)
        hx_pushes[c] = push(block, block, hx_s.at[c], hx_r.at[c], at_h)
        hx_pushes[c].start()

    def along_z(c, part):
        block = part_of(c, quarter, (here, there)[part])
        for way, where in ((0, at_z_up), (1, at_z_down)):
            zg_pushes[c, part, way] = push(block, block, zg_s.at[c, part, way], zg_r.at[c, part, way], where)
            zg_pushes[c, part, way].start()

    def share(c, slot, q):
        block = w.at[c, :, g, q]
        sib_pushes[c, slot] = push(block, block, sib_s.at[c, slot], sib_r.at[c, slot], at_core)
        sib_pushes[c, slot].start()

    def across(c):
        came = part_of(c, quarter, there)
        push(came, came, hx_s.at[c], hx_r.at[c], at_h).wait_recv()

    def onward(c):
        ways = ((0, quarter_down, at_z_up), (1, quarter_up, at_z_down))
        for part in range(2):
            for way, q, where in ways:
                block = part_of(c, q, (here, there)[part])
                push(block, block, zg_s.at[c, part, way], zg_r.at[c, part, way], where).wait_recv()
                if part == way:
                    zf_pushes[c, way] = push(block, block, zf_s.at[c, way], zf_r.at[c, way], where)
                    zf_pushes[c, way].start()
        for way, q, where in ways:
            share(c, 1 + way, q)

    def complete(c):
        for way, where in ((0, at_z_up), (1, at_z_down)):
            block = part_of(c, quarter_far, (here, there)[way])
            push(block, block, zf_s.at[c, way], zf_r.at[c, way], where).wait_recv()
        share(c, 3, quarter_far)
        for slot, q in enumerate((quarter, quarter_down, quarter_up, quarter_far)):
            block = w.at[c, :, 1 - g, q]
            push(block, block, sib_s.at[c, slot], sib_r.at[c, slot], at_core).wait_recv()

    def multiply(j, c):
        rows = pl.ds(j * 256, 256)

        def half(panel):
            return jnp.dot(
                normed[rows, :], w[c, :, panel].reshape(4 * FEAT, 256), preferred_element_type=F32
            )

        ps_out[c, j] = half(1 - l).astype(SUM_TYPE)
        ps_pushes[j, c] = push(ps_out.at[c, j], ps_in.at[c, j], ps_s.at[c, j], ps_r.at[c, j], at_x)
        ps_pushes[j, c].start()
        own[c, j] = half(l)

    def finish(j, c):
        ps_pushes[j, c].wait_recv()

        def step(i, carry):
            rows = pl.ds(pl.multiple_of(i * 64, 64), 64)
            at = pl.ds(pl.multiple_of(j * 256 + i * 64, 64), 64)
            pair = (own[c, j, rows, :] + ps_in[c, j, rows, :].astype(F32)) * D ** (-0.5)
            for head, values in ((c, pair[:, 0:128]), (3 + c, pair[:, 128:256])):
                if head < 5:
                    turned = jnp.concatenate([values[:, 64:], values[:, :64]], axis=1)
                    values = values * table_ref[0, at, :] + turned * table_ref[1, at, :]
                qkv_ref[head, at, :] = values.astype(BF16)
            return carry

        lax.fori_loop(0, 4, step, 0)

    first, second, third = ORDER
    for c in ORDER:
        update(c)
    own_pair(1)
    inverse = lax.rsqrt(wait_all(msg_r, t, r_s, r_r, peers_a) / D + 1e-05)
    for i in range(8):
        inv[i * 128:(i + 1) * 128, :] = jnp.broadcast_to(inverse[i:i + 1, :], (128, 128)).T
    for c in ORDER:
        deal(c)
    forward_pair(0)

    @pl.when(holds_prior)
    def _():
        prior_here.wait()

    @pl.when(jnp.logical_not(holds_prior))
    def _():
        prior_push.wait_recv()

    mix(first)
    along_z(first, 0)
    mix(second)
    mix(third)
    own_pair(2)
    across(first)
    along_z(first, 1)
    share(first, 0, quarter)
    along_z(second, 0)
    for j in range(4):
        normalize(y, j)
    forward_pair(1)
    across(second)
    along_z(second, 1)
    share(second, 0, quarter)
    onward(first)
    own_pair(3)
    across(third)
    along_z(third, 0)
    along_z(third, 1)
    share(third, 0, quarter)
    ready_pair(0)
    complete(first)
    multiply(0, first)
    forward_pair(2)
    ready_pair(1)
    multiply(1, first)
    onward(second)
    finish(0, first)
    finish(1, first)
    complete(second)
    multiply(0, second)
    multiply(1, second)
    forward_pair(3)
    onward(third)
    ready_pair(2)
    multiply(2, first)
    multiply(2, second)
    finish(0, second)
    finish(1, second)
    complete(third)
    multiply(0, third)
    multiply(1, third)
    multiply(2, third)
    finish(2, first)
    finish(2, second)
    ready_pair(3)
    for c in ORDER:
        multiply(3, c)
    for j in range(3):
        finish(j, third)
    for c in ORDER:
        finish(3, c)

    for copy in tok_pushes + a_pushes + b_pushes + r_pushes:
        copy.wait_send()
    for copies in (za_pushes, ya_pushes, hx_pushes, zg_pushes, zf_pushes, sib_pushes, ps_pushes):
        for copy in copies.values():
            copy.wait_send()

    @pl.when(holds_prior)
    def _():
        prior_push.wait_send()


def project(master, moment, second, gradient, prior, tokens, gain, tables):
    dma = pltpu.SemaphoreType.DMA
    vmem = pl.BlockSpec(memory_space=pltpu.VMEM)
    hbm = pl.BlockSpec(memory_space=pl.ANY)
    return pl.pallas_call(
        project_kernel,
        out_shape=(
            jax.ShapeDtypeStruct((QPK + 2, TOK, HD), BF16),
            jax.ShapeDtypeStruct((8, 128), F32),
        ),
        in_specs=[hbm] * 6 + [vmem] * 2,
        out_specs=(vmem, vmem),
        scratch_shapes=[
            pltpu.VMEM((4, TOK, FEAT), BF16),
            pltpu.VMEM((TOK, 4 * FEAT), BF16),
            pltpu.VMEM((3, 4, 2, 4, 256, 256), BF16),
            pltpu.VMEM((FEAT, COLS), F32),
            pltpu.VMEM((FEAT, COLS), F32),
            pltpu.VMEM((FEAT, COLS), F32),
            pltpu.VMEM((FEAT, COLS), BF16),
            pltpu.VMEM((TOK, 128), F32),
            pltpu.VMEM((8, 8, 128), F32),
            pltpu.VMEM((16, 8, 128), F32),
            pltpu.VMEM((8, 8, 128), F32),
            pltpu.VMEM((3, 4, 256, 128), BF16),
            pltpu.VMEM((3, 4, 256, 128), BF16),
            pltpu.VMEM((3, 4, 256, 128), BF16),
            pltpu.VMEM((4, 256, COLS), BF16),
            pltpu.VMEM((3, 4, 256, 256), F32),
            pltpu.VMEM((3, 4, 256, 256), SUM_TYPE),
            pltpu.VMEM((3, 4, 256, 256), SUM_TYPE),
            dma((6,)),
            dma((2, PIECES)), dma((2, PIECES)), dma((2, 4)), dma((2, 4)),
            dma((7,)), dma((7,)), dma((15,)), dma((15,)), dma((7,)), dma((7,)),
            dma, dma,
            dma((3, 3)), dma((3, 3)), dma((3, 3)), dma((3, 3)), dma((3,)), dma((3,)),
            dma((3, 2, 2)), dma((3, 2, 2)), dma((3, 2)), dma((3, 2)),
            dma((3, 4)), dma((3, 4)), dma((3, 4)), dma((3, 4)),
        ],
        compiler_params=pltpu.CompilerParams(
            collective_id=0, has_side_effects=True, vmem_limit_bytes=60 * 1024 * 1024
        ),
        cost_estimate=pl.CostEstimate(
            flops=2 * TOK * D * 768, bytes_accessed=24 * 1024 * 1024, transcendentals=0
        ),
    )(master, moment, second, gradient, prior.reshape(8, 4, 256, 768), tokens, gain, tables)


BLOCK = 256


def attend_kernel(
    qkv_ref, clip_ref, seg_ref, master_ref, moment_ref, second_ref, grad_ref,
    new_master_ref, new_moment_ref, new_second_ref, out_ref,
):
    place = pl.program_id(0)

    def adam_rows(i, carry):
        rows = pl.ds(pl.multiple_of(i * 32, 32), 32)
        clip = jnp.concatenate([clip_ref[0:1, :]] * 3, axis=1)
        new_master, new_moment, new_second = adam(
            master_ref[rows, :], moment_ref[rows, :], second_ref[rows, :], grad_ref[rows, :].astype(F32), clip
        )
        new_master_ref[rows, :] = new_master
        new_moment_ref[rows, :] = new_moment
        new_second_ref[rows, :] = new_second
        return carry

    lax.fori_loop(0, BLOCK // 32, adam_rows, 0)

    for q in range(TOK // BLOCK):
        @pl.when(place == q)
        def _(q=q):
            first = max(0, q - 2) * BLOCK
            last = (q + 1) * BLOCK
            width = last - first
            segments = seg_ref[0:1, :].astype(F32)
            column = jnp.concatenate(
                [
                    jnp.broadcast_to(segments[:, s:s + 128], (128, 128)).T
                    for s in range(q * BLOCK, last, 128)
                ],
                axis=0,
            )
            same = jnp.concatenate([column] * (width // 128), axis=1) == segments[:, first:last]
            at_query = lax.broadcasted_iota(jnp.int32, (BLOCK, width), 0) + q * BLOCK
            at_key = lax.broadcasted_iota(jnp.int32, (BLOCK, width), 1) + first
            allowed = same & (at_query >= at_key)
            for head in range(QPK):
                scores = lax.dot_general(
                    qkv_ref[head, q * BLOCK:last, :], qkv_ref[QPK, first:last, :],
                    (((1,), (1,)), ((), ())), preferred_element_type=F32,
                ) * HD ** (-0.5)
                scores = jnp.where(allowed, scores, -jnp.inf)
                weights = jnp.exp(scores - jnp.max(scores, axis=1, keepdims=True))
                weights = (weights / jnp.sum(weights, axis=1, keepdims=True)).astype(BF16)
                out_ref[:, head * HD:(head + 1) * HD] = jnp.dot(
                    weights, qkv_ref[QPK + 1, first:last, :], preferred_element_type=F32
                ).astype(BF16)


def attend(qkv, clip, segments, master, moment, second, gradient):
    steps = TOK // BLOCK
    rows = pl.BlockSpec((BLOCK, COLS), lambda i: (i, 0))
    return pl.pallas_call(
        attend_kernel,
        grid=(steps,),
        out_shape=(
            jax.ShapeDtypeStruct((FEAT, COLS), F32),
            jax.ShapeDtypeStruct((FEAT, COLS), F32),
            jax.ShapeDtypeStruct((FEAT, COLS), F32),
            jax.ShapeDtypeStruct((TOK, QPK * HD), BF16),
        ),
        in_specs=[
            pl.BlockSpec((QPK + 2, TOK, HD), lambda i: (0, 0, 0)),
            pl.BlockSpec((8, 128), lambda i: (0, 0)),
            pl.BlockSpec((1, TOK), lambda i: (0, 0)),
            rows, rows, rows, rows,
        ],
        out_specs=(rows, rows, rows, pl.BlockSpec((BLOCK, QPK * HD), lambda i: (i, 0))),
        compiler_params=pltpu.CompilerParams(vmem_limit_bytes=48 * 1024 * 1024),
    )(qkv, clip, segments, master, moment, second, gradient)


def shards(master, moment, second, gradient, prior_weights, tokens, norm_gain, segment_ids):
    qkv, clip = project(
        master, moment, second, gradient, prior_weights, tokens[0], norm_gain.reshape(8, 1, FEAT),
        jnp.asarray(rotary_tables()),
    )
    new_master, new_moment, new_second, attended = attend(
        qkv, clip, segment_ids, master, moment, second, gradient
    )
    return (new_master, new_moment, new_second, attended[None])


def solution(mesh):
    in_specs = (
        P("tensor", ("group", "fsdp")),
        P("tensor", ("group", "fsdp")),
        P("tensor", ("group", "fsdp")),
        P("tensor", ("group", "fsdp")),
        P(None, "tensor"),
        P(("group", "fsdp"), None, "tensor"),
        P(),
        P(("group", "fsdp"), None),
    )
    out_specs = (
        P("tensor", ("group", "fsdp")),
        P("tensor", ("group", "fsdp")),
        P("tensor", ("group", "fsdp")),
        P(("group", "fsdp"), None, "tensor"),
    )
    return jax.shard_map(shards, mesh=mesh, in_specs=in_specs, out_specs=out_specs, check_vma=False)
```

```python
import functools
import math

import jax
import jax.numpy as jnp
import numpy as np
from jax import lax
from jax.experimental import pallas as pl
from jax.experimental.pallas import tpu as pltpu
from jax.sharding import PartitionSpec as P

D = 8192
HD = 128
QPK = 4
QKV = 6144

learn_rate = 0.01
decay_rate = 0.1
clip_rms = 0.25
first_fix = 1.0 - math.exp(200.0 * math.log(0.9))
second_fix = 1.0 - math.exp(200.0 * math.log(0.95))
mix_share = 0.6

MESH = pl.DeviceIdType.MESH
F32 = jnp.float32
BF16 = jnp.bfloat16
SUM_TYPE = BF16
TOK = 1024
FEAT = 1024
COLS = 384
PIECES = 8
PIECE = TOK // PIECES
ORDER = (2, 1, 0)


def rotary_tables():
    places = np.arange(TOK).astype(np.float32)
    lanes = np.arange(HD // 2).astype(np.float32)
    frequencies = np.power(500000.0, -(lanes * np.float32(2.0) / np.float32(HD)).astype(np.float64))
    angles = places[:, None] * frequencies.astype(np.float32)[None, :]
    cosine = np.cos(angles.astype(np.float64)).astype(np.float32)
    sine = np.sin(angles.astype(np.float64)).astype(np.float32)
    return np.stack(
        [np.concatenate([cosine, cosine], 1), np.concatenate([-sine, sine], 1)]
    ).astype(np.float32)


def adam(master, moment, second, grad, clip):
    clipped = clip * grad
    new_moment = 0.9 * moment + 0.1 * clipped
    new_second = 0.95 * second + 0.05 * clipped * clipped
    update = (
        new_moment / first_fix / (jnp.sqrt(new_second / second_fix) + 1e-08) + decay_rate * master
    )
    return master - learn_rate * update, new_moment, new_second


def push(src, dst, send, recv, where):
    return pltpu.make_async_remote_copy(
        src_ref=src, dst_ref=dst, send_sem=send, recv_sem=recv, device_id=where, device_id_type=MESH
    )


def project_kernel(
    master_ref, moment_ref, second_ref, grad_ref, prior_ref, tok_ref, gain_ref, table_ref, seg_ref,
    out_ref, clip_ref,
    raw, normed, w, mas, mom, sec, gra, inv, msg_a, msg_b, msg_r, z_out, z_in, y_in, pri, own, ps_out, ps_in, qkv, bias,
    load_sem, tok_s, tok_r, fwd_s, fwd_r, a_s, a_r, b_s, b_r, r_s, r_r, pri_s, pri_r,
    za_s, za_r, ya_s, ya_r, hx_s, hx_r, zg_s, zg_r, zf_s, zf_r, sib_s, sib_r, ps_s, ps_r,
):
    g = lax.axis_index("group")
    f = lax.axis_index("fsdp")
    t = lax.axis_index("tensor")
    z, h = f // 2, f % 2
    l, y = t // 4, t % 4
    y_up, y_down, y_far = (y + 1) % 4, (y + 3) % 4, (y + 2) % 4
    z_up, z_down, z_far = (z + 1) % 4, (z + 3) % 4, (z + 2) % 4
    at_y_up, at_y_down = (g, f, l * 4 + y_up), (g, f, l * 4 + y_down)
    at_z_up, at_z_down = (g, z_up * 2 + h, t), (g, z_down * 2 + h, t)
    at_x = (g, f, (1 - l) * 4 + y)
    at_h = (g, z * 2 + (1 - h), t)
    at_core = (1 - g, f, t)
    mine = g * 8 + f
    quarter = (z + 4 - y) % 4
    quarter_up, quarter_down, quarter_far = (quarter + 1) % 4, (quarter + 3) % 4, (quarter + 2) % 4

    loads = [
        pltpu.make_async_copy(grad_ref, gra, load_sem.at[0]),
        pltpu.make_async_copy(tok_ref, raw.at[y], load_sem.at[1]),
        pltpu.make_async_copy(master_ref, mas, load_sem.at[2]),
        pltpu.make_async_copy(moment_ref, mom, load_sem.at[3]),
        pltpu.make_async_copy(second_ref, sec, load_sem.at[4]),
    ]
    for load in loads:
        load.start()
    prior_cols = pl.ds(pl.multiple_of(h * COLS, 128), COLS)
    prior_here = pltpu.make_async_copy(
        prior_ref.at[pl.ds(l * 4, 4), quarter, :, prior_cols], pri, load_sem.at[5]
    )
    prior_push = push(
        prior_ref.at[pl.ds((1 - l) * 4, 4), quarter, :, prior_cols], pri, pri_s, pri_r, at_x
    )
    holds_prior = g == l

    peers_a = [(g, f, (t + d) % 8) for d in range(1, 8)]
    places_b = [(mine + d) % 16 for d in range(1, 16)]
    peers_b = [(place // 8, place % 8, t) for place in places_b]

    barrier = pltpu.get_barrier_semaphore()
    for peer in peers_a + peers_b:
        pl.semaphore_signal(barrier, inc=1, device_id=peer, device_id_type=MESH)

    loads[0].wait()

    def grad_sum(i, total):
        v = gra[pl.ds(pl.multiple_of(i * 64, 64), 64), :].astype(F32)
        return total + jnp.sum((v * v).reshape(8, 8, COLS), axis=0)

    total = lax.fori_loop(0, FEAT // 64, grad_sum, jnp.zeros((8, COLS), F32))
    msg_a[t] = total[:, 0:128] + total[:, 128:256] + total[:, 256:384]
    pl.semaphore_wait(barrier, 22)

    def send_all(msg, slot, send, recv, peers):
        copies = [push(msg.at[slot], msg.at[slot], send.at[d], recv.at[d], peer) for d, peer in enumerate(peers)]
        for copy in copies:
            copy.start()
        return copies

    def wait_all(msg, slot, send, recv, peers):
        count = len(peers) + 1
        for d, peer in enumerate(peers):
            source = (slot + count - 1 - d) % count
            push(msg.at[source], msg.at[source], send.at[d], recv.at[d], peer).wait_recv()
        sums = msg[0]
        for s in range(1, count):
            sums = sums + msg[s]
        return sums

    a_pushes = send_all(msg_a, t, a_s, a_r, peers_a)

    tok_pushes = []

    def tok_rows(piece):
        return pl.ds(piece * PIECE, PIECE)

    def own_pair(j):
        for piece in (2 * j, 2 * j + 1):
            for way, where in ((0, at_y_up), (1, at_y_down)):
                copy = push(
                    tok_ref.at[tok_rows(piece), :], raw.at[y, tok_rows(piece), :],
                    tok_s.at[way, piece], tok_r.at[way, piece], where,
                )
                copy.start()
                tok_pushes.append(copy)

    def forward_pair(j):
        for way, source, where in ((0, y_down, at_y_up), (1, y_up, at_y_down)):
            piece = 2 * j + way
            block = raw.at[source, tok_rows(piece), :]
            push(block, block, tok_s.at[way, piece], tok_r.at[way, piece], where).wait_recv()
            copy = push(block, block, fwd_s.at[way, j], fwd_r.at[way, j], where)
            copy.start()
            tok_pushes.append(copy)

    def normalize(block, j):
        gain = gain_ref[l * 4 + block]
        cols = pl.ds(pl.multiple_of(block * FEAT, FEAT), FEAT)

        def step(i, carry):
            rows = pl.ds(pl.multiple_of(j * 256 + i * 32, 32), 32)
            scale = jnp.concatenate([inv[rows, :]] * (FEAT // 128), axis=1)
            normed[rows, cols] = (raw[block, rows, :].astype(F32) * scale * gain).astype(BF16)
            return carry

        lax.fori_loop(0, 8, step, 0)

    def ready_pair(j):
        for way, source, where in ((0, y_down, at_y_up), (1, y_up, at_y_down)):
            piece = 2 * j + 1 - way
            block = raw.at[source, tok_rows(piece), :]
            push(block, block, tok_s.at[way, piece], tok_r.at[way, piece], where).wait_recv()
        normalize(y_down, j)
        normalize(y_up, j)
        for way, where in ((0, at_y_up), (1, at_y_down)):
            block = raw.at[y_far, tok_rows(2 * j + way), :]
            push(block, block, fwd_s.at[way, j], fwd_r.at[way, j], where).wait_recv()
        normalize(y_far, j)

    loads[1].wait()
    for i in range(8):
        part = jnp.zeros((128, 128), F32)
        for j in range(FEAT // 128):
            v = raw[y, i * 128:(i + 1) * 128, j * 128:(j + 1) * 128].astype(F32)
            part = part + v * v
        msg_r[t, i:i + 1, :] = jnp.sum(part.T, axis=0, keepdims=True)

    msg_b[mine] = wait_all(msg_a, t, a_s, a_r, peers_a)
    b_pushes = send_all(msg_b, mine, b_s, b_r, peers_b)
    own_pair(0)
    sums = wait_all(msg_b, mine, b_s, b_r, peers_b)
    overall = jnp.broadcast_to(jnp.sum(sums, keepdims=True), (8, 128))
    clip_ref[...] = jnp.minimum(1.0, clip_rms * math.sqrt(D * QKV) / (jnp.sqrt(overall) + 1e-06))

    for load in loads[2:]:
        load.wait()
    za_pushes, ya_pushes, hx_pushes, zg_pushes, zf_pushes, sib_pushes, ps_pushes = {}, {}, {}, {}, {}, {}, {}

    def update(c):
        cols = slice(c * 128, (c + 1) * 128)

        def step(i, carry):
            rows = pl.ds(pl.multiple_of(i * 64, 64), 64)
            updated, _, _ = adam(
                mas[rows, cols], mom[rows, cols], sec[rows, cols], gra[rows, cols].astype(F32), clip_ref[0:1, :]
            )
            z_out[c, i // 4, pl.ds(pl.multiple_of(i % 4 * 64, 64), 64), :] = updated.astype(BF16)
            return carry

        lax.fori_loop(0, FEAT // 64, step, 0)
        for d in range(1, 4):
            za_pushes[c, d] = push(
                z_out.at[c, d], z_in.at[c, d], za_s.at[c, d - 1], za_r.at[c, d - 1], (g, (z + d) % 4 * 2 + h, t)
            )
            za_pushes[c, d].start()
        z_in[c, 0] = z_out[c, 0]

    def deal(c):
        for d in range(1, 4):
            za_pushes[c, d].wait_recv()
        for d in range(1, 4):
            other = (y + d) % 4
            ya_pushes[c, d] = push(
                z_in.at[c, (z + 4 - other) % 4], y_in.at[c, y], ya_s.at[c, d - 1], ya_r.at[c, d - 1],
                (g, f, l * 4 + other),
            )
            ya_pushes[c, d].start()
        y_in[c, y] = z_in[c, quarter]

    here = pl.ds(pl.multiple_of(h * 128, 128), 128)
    there = pl.ds(pl.multiple_of((1 - h) * 128, 128), 128)

    def part_of(c, q, cols):
        return w.at[c, :, g, q, :, cols]

    def mix(c):
        for d in range(1, 4):
            block = y_in.at[c, (y + 4 - d) % 4]
            push(block, block, ya_s.at[c, d - 1], ya_r.at[c, d - 1], (g, f, l * 4 + (y + d) % 4)).wait_recv()
        for block in range(4):
            policy = y_in[c, block].astype(F32)
            prior = pri[block, :, c * 128:(c + 1) * 128].astype(F32)
            w[c, block, g, quarter, :, here] = (mix_share * policy + (1.0 - mix_share) * prior).astype(BF16)
        block = part_of(c, quarter, here)
        hx_pushes[c] = push(block, block, hx_s.at[c], hx_r.at[c], at_h)
        hx_pushes[c].start()

    def along_z(c, part):
        block = part_of(c, quarter, (here, there)[part])
        for way, where in ((0, at_z_up), (1, at_z_down)):
            zg_pushes[c, part, way] = push(block, block, zg_s.at[c, part, way], zg_r.at[c, part, way], where)
            zg_pushes[c, part, way].start()

    def share(c, slot, q):
        block = w.at[c, :, g, q]
        sib_pushes[c, slot] = push(block, block, sib_s.at[c, slot], sib_r.at[c, slot], at_core)
        sib_pushes[c, slot].start()

    def across(c):
        came = part_of(c, quarter, there)
        push(came, came, hx_s.at[c], hx_r.at[c], at_h).wait_recv()

    def onward(c):
        ways = ((0, quarter_down, at_z_up), (1, quarter_up, at_z_down))
        for part in range(2):
            for way, q, where in ways:
                block = part_of(c, q, (here, there)[part])
                push(block, block, zg_s.at[c, part, way], zg_r.at[c, part, way], where).wait_recv()
                if part == way:
                    zf_pushes[c, way] = push(block, block, zf_s.at[c, way], zf_r.at[c, way], where)
                    zf_pushes[c, way].start()
        for way, q, where in ways:
            share(c, 1 + way, q)

    def complete(c):
        for way, where in ((0, at_z_up), (1, at_z_down)):
            block = part_of(c, quarter_far, (here, there)[way])
            push(block, block, zf_s.at[c, way], zf_r.at[c, way], where).wait_recv()
        share(c, 3, quarter_far)
        for slot, q in enumerate((quarter, quarter_down, quarter_up, quarter_far)):
            block = w.at[c, :, 1 - g, q]
            push(block, block, sib_s.at[c, slot], sib_r.at[c, slot], at_core).wait_recv()

    def multiply(j, c):
        rows = pl.ds(j * 256, 256)

        def half(panel):
            return jnp.dot(
                normed[rows, :], w[c, :, panel].reshape(4 * FEAT, 256), preferred_element_type=F32
            )

        ps_out[c, j] = half(1 - l).astype(SUM_TYPE)
        ps_pushes[j, c] = push(ps_out.at[c, j], ps_in.at[c, j], ps_s.at[c, j], ps_r.at[c, j], at_x)
        ps_pushes[j, c].start()
        own[c, j] = half(l)

    def finish(j, c):
        ps_pushes[j, c].wait_recv()

        def step(i, carry):
            rows = pl.ds(pl.multiple_of(i * 64, 64), 64)
            at = pl.ds(pl.multiple_of(j * 256 + i * 64, 64), 64)
            pair = (own[c, j, rows, :] + ps_in[c, j, rows, :].astype(F32)) * D ** (-0.5)
            for head, values in ((c, pair[:, 0:128]), (3 + c, pair[:, 128:256])):
                if head < 5:
                    turned = jnp.concatenate([values[:, 64:], values[:, :64]], axis=1)
                    values = values * table_ref[0, at, :] + turned * table_ref[1, at, :]
                qkv[head, at, :] = values.astype(BF16)
            return carry

        lax.fori_loop(0, 4, step, 0)

    def key_range(j):
        return max(0, j - 2) * 256, (j + 1) * 256

    def mask(j):
        low, high = key_range(j)
        segments = seg_ref[0:1, :].astype(F32)
        column = jnp.concatenate(
            [
                jnp.broadcast_to(segments[:, s:s + 128], (128, 128)).T
                for s in range(j * 256, high, 128)
            ],
            axis=0,
        )
        same = jnp.concatenate([column] * ((high - low) // 128), axis=1) == segments[:, low:high]
        at_query = lax.broadcasted_iota(jnp.int32, (256, high - low), 0) + j * 256
        at_key = lax.broadcasted_iota(jnp.int32, (256, high - low), 1) + low
        bias[j, :, 0:high - low] = jnp.where(same & (at_query >= at_key), 0.0, -jnp.inf)

    def attend(j, head):
        low, high = key_range(j)
        scores = lax.dot_general(
            qkv[head, j * 256:high, :], qkv[QPK, low:high, :],
            (((1,), (1,)), ((), ())), preferred_element_type=F32,
        ) * HD ** (-0.5) + bias[j, :, 0:high - low]
        weights = jnp.exp(scores - jnp.max(scores, axis=1, keepdims=True))
        weights = (weights / jnp.sum(weights, axis=1, keepdims=True)).astype(BF16)
        out_ref[j * 256:high, head * HD:(head + 1) * HD] = jnp.dot(
            weights, qkv[QPK + 1, low:high, :], preferred_element_type=F32
        ).astype(BF16)

    first, second, third = ORDER

    def row_scales():
        inverse = lax.rsqrt(wait_all(msg_r, t, r_s, r_r, peers_a) / D + 1e-05)
        for i in range(8):
            inv[i * 128:(i + 1) * 128, :] = jnp.broadcast_to(inverse[i:i + 1, :], (128, 128)).T

    def prior_ready():
        @pl.when(holds_prior)
        def _():
            prior_here.wait()

        @pl.when(jnp.logical_not(holds_prior))
        def _():
            prior_push.wait_recv()

    update(first)

    @pl.when(holds_prior)
    def _():
        prior_push.start()
        prior_here.start()

    update(second)
    update(third)
    r_pushes = send_all(msg_r, t, r_s, r_r, peers_a)
    deal(first)
    prior_ready()
    mix(first)
    along_z(first, 0)
    deal(second)
    deal(third)
    own_pair(1)
    row_scales()
    mix(second)
    forward_pair(0)
    mix(third)
    across(first)
    along_z(first, 1)
    share(first, 0, quarter)
    along_z(second, 0)
    own_pair(2)
    for j in range(4):
        normalize(y, j)
        mask(j)
    across(second)
    along_z(second, 1)
    share(second, 0, quarter)
    onward(first)
    forward_pair(1)
    across(third)
    share(third, 0, quarter)
    along_z(third, 0)
    along_z(third, 1)
    ready_pair(0)
    complete(first)
    multiply(0, first)
    own_pair(3)
    ready_pair(1)
    multiply(1, first)
    onward(second)
    finish(0, first)
    forward_pair(2)
    complete(second)
    multiply(0, second)
    multiply(1, second)
    onward(third)
    finish(1, first)
    ready_pair(2)
    multiply(2, first)
    multiply(2, second)
    finish(0, second)
    finish(1, second)
    attend(0, 1)
    attend(0, 2)
    forward_pair(3)
    complete(third)
    multiply(0, third)
    multiply(1, third)
    multiply(2, third)
    attend(1, 1)
    attend(1, 2)
    finish(2, first)
    finish(2, second)
    ready_pair(3)
    for c in ORDER:
        multiply(3, c)
    attend(2, 1)
    attend(2, 2)
    for j in range(3):
        finish(j, third)
        attend(j, 0)
        attend(j, 3)
    finish(3, first)
    finish(3, second)
    attend(3, 1)
    attend(3, 2)
    finish(3, third)
    attend(3, 0)
    attend(3, 3)

    for copy in tok_pushes + a_pushes + b_pushes + r_pushes:
        copy.wait_send()
    for copies in (za_pushes, ya_pushes, hx_pushes, zg_pushes, zf_pushes, sib_pushes, ps_pushes):
        for copy in copies.values():
            copy.wait_send()

    @pl.when(holds_prior)
    def _():
        prior_push.wait_send()


def project(master, moment, second, gradient, prior, tokens, gain, tables, segments):
    dma = pltpu.SemaphoreType.DMA
    vmem = pl.BlockSpec(memory_space=pltpu.VMEM)
    hbm = pl.BlockSpec(memory_space=pl.ANY)
    return pl.pallas_call(
        project_kernel,
        out_shape=(
            jax.ShapeDtypeStruct((TOK, QPK * HD), BF16),
            jax.ShapeDtypeStruct((8, 128), F32),
        ),
        in_specs=[hbm] * 6 + [vmem] * 3,
        out_specs=(vmem, vmem),
        scratch_shapes=[
            pltpu.VMEM((4, TOK, FEAT), BF16),
            pltpu.VMEM((TOK, 4 * FEAT), BF16),
            pltpu.VMEM((3, 4, 2, 4, 256, 256), BF16),
            pltpu.VMEM((FEAT, COLS), F32),
            pltpu.VMEM((FEAT, COLS), F32),
            pltpu.VMEM((FEAT, COLS), F32),
            pltpu.VMEM((FEAT, COLS), BF16),
            pltpu.VMEM((TOK, 128), F32),
            pltpu.VMEM((8, 8, 128), F32),
            pltpu.VMEM((16, 8, 128), F32),
            pltpu.VMEM((8, 8, 128), F32),
            pltpu.VMEM((3, 4, 256, 128), BF16),
            pltpu.VMEM((3, 4, 256, 128), BF16),
            pltpu.VMEM((3, 4, 256, 128), BF16),
            pltpu.VMEM((4, 256, COLS), BF16),
            pltpu.VMEM((3, 4, 256, 256), F32),
            pltpu.VMEM((3, 4, 256, 256), SUM_TYPE),
            pltpu.VMEM((3, 4, 256, 256), SUM_TYPE),
            pltpu.VMEM((QPK + 2, TOK, HD), BF16),
            pltpu.VMEM((4, 256, 768), F32),
            dma((6,)),
            dma((2, PIECES)), dma((2, PIECES)), dma((2, 4)), dma((2, 4)),
            dma((7,)), dma((7,)), dma((15,)), dma((15,)), dma((7,)), dma((7,)),
            dma, dma,
            dma((3, 3)), dma((3, 3)), dma((3, 3)), dma((3, 3)), dma((3,)), dma((3,)),
            dma((3, 2, 2)), dma((3, 2, 2)), dma((3, 2)), dma((3, 2)),
            dma((3, 4)), dma((3, 4)), dma((3, 4)), dma((3, 4)),
        ],
        compiler_params=pltpu.CompilerParams(
            collective_id=0, has_side_effects=True, vmem_limit_bytes=60 * 1024 * 1024
        ),
        cost_estimate=pl.CostEstimate(
            flops=2 * TOK * D * 768, bytes_accessed=24 * 1024 * 1024, transcendentals=0
        ),
    )(master, moment, second, gradient, prior.reshape(8, 4, 256, 768), tokens, gain, tables, segments)


BLOCK = 256


def outputs_kernel(
    clip_ref, master_ref, moment_ref, second_ref, grad_ref, attended_ref,
    new_master_ref, new_moment_ref, new_second_ref, out_ref,
):
    def step(i, carry):
        rows = pl.ds(pl.multiple_of(i * 32, 32), 32)
        clip = jnp.concatenate([clip_ref[0:1, :]] * 3, axis=1)
        new_master, new_moment, new_second = adam(
            master_ref[rows, :], moment_ref[rows, :], second_ref[rows, :], grad_ref[rows, :].astype(F32), clip
        )
        new_master_ref[rows, :] = new_master
        new_moment_ref[rows, :] = new_moment
        new_second_ref[rows, :] = new_second
        return carry

    lax.fori_loop(0, BLOCK // 32, step, 0)
    out_ref[...] = attended_ref[...]


def outputs(clip, master, moment, second, gradient, attended):
    rows = pl.BlockSpec((BLOCK, COLS), lambda i: (i, 0))
    wide = pl.BlockSpec((BLOCK, QPK * HD), lambda i: (i, 0))
    return pl.pallas_call(
        outputs_kernel,
        grid=(TOK // BLOCK,),
        out_shape=(
            jax.ShapeDtypeStruct((FEAT, COLS), F32),
            jax.ShapeDtypeStruct((FEAT, COLS), F32),
            jax.ShapeDtypeStruct((FEAT, COLS), F32),
            jax.ShapeDtypeStruct((TOK, QPK * HD), BF16),
        ),
        in_specs=[pl.BlockSpec((8, 128), lambda i: (0, 0)), rows, rows, rows, rows, wide],
        out_specs=(rows, rows, rows, wide),
        compiler_params=pltpu.CompilerParams(vmem_limit_bytes=32 * 1024 * 1024),
    )(clip, master, moment, second, gradient, attended)


def shards(master, moment, second, gradient, prior_weights, tokens, norm_gain, segment_ids):
    attended, clip = project(
        master, moment, second, gradient, prior_weights, tokens[0], norm_gain.reshape(8, 1, FEAT),
        jnp.asarray(rotary_tables()), segment_ids,
    )
    new_master, new_moment, new_second, attended = outputs(
        clip, master, moment, second, gradient, attended
    )
    return (new_master, new_moment, new_second, attended[None])


def solution(mesh):
    in_specs = (
        P("tensor", ("group", "fsdp")),
        P("tensor", ("group", "fsdp")),
        P("tensor", ("group", "fsdp")),
        P("tensor", ("group", "fsdp")),
        P(None, "tensor"),
        P(("group", "fsdp"), None, "tensor"),
        P(),
        P(("group", "fsdp"), None),
    )
    out_specs = (
        P("tensor", ("group", "fsdp")),
        P("tensor", ("group", "fsdp")),
        P("tensor", ("group", "fsdp")),
        P(("group", "fsdp"), None, "tensor"),
    )
    return jax.shard_map(shards, mesh=mesh, in_specs=in_specs, out_specs=out_specs, check_vma=False)
```

```python
import functools
import math

import jax
import jax.numpy as jnp
import numpy as np
from jax import lax
from jax.experimental import pallas as pl
from jax.experimental.pallas import tpu as pltpu
from jax.sharding import PartitionSpec as P

D = 8192
HD = 128
QPK = 4
QKV = 6144

learn_rate = 0.01
decay_rate = 0.1
clip_rms = 0.25
first_fix = 1.0 - math.exp(200.0 * math.log(0.9))
second_fix = 1.0 - math.exp(200.0 * math.log(0.95))
mix_share = 0.6

MESH = pl.DeviceIdType.MESH
F32 = jnp.float32
BF16 = jnp.bfloat16
SUM_TYPE = BF16
TOK = 1024
FEAT = 1024
COLS = 384
GROUPS = ((0, 256), (256, 256), (512, 256), (768, 128), (896, 128))
ORDER = (2, 1, 0)


def rotary_tables():
    places = np.arange(TOK).astype(np.float32)
    lanes = np.arange(HD // 2).astype(np.float32)
    frequencies = np.power(500000.0, -(lanes * np.float32(2.0) / np.float32(HD)).astype(np.float64))
    angles = places[:, None] * frequencies.astype(np.float32)[None, :]
    cosine = np.cos(angles.astype(np.float64)).astype(np.float32)
    sine = np.sin(angles.astype(np.float64)).astype(np.float32)
    return np.stack(
        [np.concatenate([cosine, cosine], 1), np.concatenate([-sine, sine], 1)]
    ).astype(np.float32)


def adam(master, moment, second, grad, clip):
    clipped = clip * grad
    new_moment = 0.9 * moment + 0.1 * clipped
    new_second = 0.95 * second + 0.05 * clipped * clipped
    update = (
        new_moment / first_fix / (jnp.sqrt(new_second / second_fix) + 1e-08) + decay_rate * master
    )
    return master - learn_rate * update, new_moment, new_second


def push(src, dst, send, recv, where):
    return pltpu.make_async_remote_copy(
        src_ref=src, dst_ref=dst, send_sem=send, recv_sem=recv, device_id=where, device_id_type=MESH
    )


def project_kernel(
    master_ref, moment_ref, second_ref, grad_ref, prior_ref, tok_ref, gain_ref, table_ref, seg_ref,
    out_ref, clip_ref,
    raw, normed, w, mas, mom, sec, gra, inv, msg_a, msg_b, msg_r, z_out, z_in, y_in, pri, own, ps_out, ps_in, qkv, bias,
    load_sem, tok_s, tok_r, fwd_s, fwd_r, a_s, a_r, b_s, b_r, r_s, r_r, pri_s, pri_r,
    za_s, za_r, ya_s, ya_r, hx_s, hx_r, zg_s, zg_r, zf_s, zf_r, sib_s, sib_r, ps_s, ps_r,
):
    g = lax.axis_index("group")
    f = lax.axis_index("fsdp")
    t = lax.axis_index("tensor")
    z, h = f // 2, f % 2
    l, y = t // 4, t % 4
    y_up, y_down, y_far = (y + 1) % 4, (y + 3) % 4, (y + 2) % 4
    z_up, z_down, z_far = (z + 1) % 4, (z + 3) % 4, (z + 2) % 4
    at_y_up, at_y_down = (g, f, l * 4 + y_up), (g, f, l * 4 + y_down)
    at_z_up, at_z_down = (g, z_up * 2 + h, t), (g, z_down * 2 + h, t)
    at_x = (g, f, (1 - l) * 4 + y)
    at_h = (g, z * 2 + (1 - h), t)
    at_core = (1 - g, f, t)
    mine = g * 8 + f
    quarter = (z + 4 - y) % 4
    quarter_up, quarter_down, quarter_far = (quarter + 1) % 4, (quarter + 3) % 4, (quarter + 2) % 4

    loads = [
        pltpu.make_async_copy(grad_ref, gra, load_sem.at[0]),
        pltpu.make_async_copy(tok_ref, raw.at[y], load_sem.at[1]),
        pltpu.make_async_copy(master_ref, mas, load_sem.at[2]),
        pltpu.make_async_copy(moment_ref, mom, load_sem.at[3]),
        pltpu.make_async_copy(second_ref, sec, load_sem.at[4]),
    ]
    for load in loads:
        load.start()
    prior_cols = pl.ds(pl.multiple_of(h * COLS, 128), COLS)
    prior_here = pltpu.make_async_copy(
        prior_ref.at[pl.ds(l * 4, 4), quarter, :, prior_cols], pri, load_sem.at[5]
    )
    prior_push = push(
        prior_ref.at[pl.ds((1 - l) * 4, 4), quarter, :, prior_cols], pri, pri_s, pri_r, at_x
    )
    holds_prior = g == l

    peers_a = [(g, f, (t + d) % 8) for d in range(1, 8)]
    places_b = [(mine + d) % 16 for d in range(1, 16)]
    peers_b = [(place // 8, place % 8, t) for place in places_b]

    barrier = pltpu.get_barrier_semaphore()
    for peer in peers_a + peers_b:
        pl.semaphore_signal(barrier, inc=1, device_id=peer, device_id_type=MESH)

    loads[0].wait()

    def grad_sum(i, total):
        v = gra[pl.ds(pl.multiple_of(i * 64, 64), 64), :].astype(F32)
        return total + jnp.sum((v * v).reshape(8, 8, COLS), axis=0)

    total = lax.fori_loop(0, FEAT // 64, grad_sum, jnp.zeros((8, COLS), F32))
    msg_a[t] = total[:, 0:128] + total[:, 128:256] + total[:, 256:384]
    pl.semaphore_wait(barrier, 22)

    def send_all(msg, slot, send, recv, peers):
        copies = [push(msg.at[slot], msg.at[slot], send.at[d], recv.at[d], peer) for d, peer in enumerate(peers)]
        for copy in copies:
            copy.start()
        return copies

    def wait_all(msg, slot, send, recv, peers):
        count = len(peers) + 1
        for d, peer in enumerate(peers):
            source = (slot + count - 1 - d) % count
            push(msg.at[source], msg.at[source], send.at[d], recv.at[d], peer).wait_recv()
        sums = msg[0]
        for s in range(1, count):
            sums = sums + msg[s]
        return sums

    a_pushes = send_all(msg_a, t, a_s, a_r, peers_a)

    tok_pushes = []

    def tok_rows(piece):
        start, count = GROUPS[piece // 2]
        return pl.ds(start + piece % 2 * (count // 2), count // 2)

    def own_pair(j):
        for piece in (2 * j, 2 * j + 1):
            for way, where in ((0, at_y_up), (1, at_y_down)):
                copy = push(
                    tok_ref.at[tok_rows(piece), :], raw.at[y, tok_rows(piece), :],
                    tok_s.at[way, piece], tok_r.at[way, piece], where,
                )
                copy.start()
                tok_pushes.append(copy)

    def forward_pair(j):
        for way, source, where in ((0, y_down, at_y_up), (1, y_up, at_y_down)):
            piece = 2 * j + way
            block = raw.at[source, tok_rows(piece), :]
            push(block, block, tok_s.at[way, piece], tok_r.at[way, piece], where).wait_recv()
            copy = push(block, block, fwd_s.at[way, j], fwd_r.at[way, j], where)
            copy.start()
            tok_pushes.append(copy)

    def normalize(block, j):
        gain = gain_ref[l * 4 + block]
        cols = pl.ds(pl.multiple_of(block * FEAT, FEAT), FEAT)
        start, count = GROUPS[j]

        def step(i, carry):
            rows = pl.ds(pl.multiple_of(start + i * 32, 32), 32)
            scale = jnp.concatenate([inv[rows, :]] * (FEAT // 128), axis=1)
            normed[rows, cols] = (raw[block, rows, :].astype(F32) * scale * gain).astype(BF16)
            return carry

        lax.fori_loop(0, count // 32, step, 0)

    def ready_pair(j):
        for way, source, where in ((0, y_down, at_y_up), (1, y_up, at_y_down)):
            piece = 2 * j + 1 - way
            block = raw.at[source, tok_rows(piece), :]
            push(block, block, tok_s.at[way, piece], tok_r.at[way, piece], where).wait_recv()
        normalize(y_down, j)
        normalize(y_up, j)
        for way, where in ((0, at_y_up), (1, at_y_down)):
            block = raw.at[y_far, tok_rows(2 * j + way), :]
            push(block, block, fwd_s.at[way, j], fwd_r.at[way, j], where).wait_recv()
        normalize(y_far, j)

    loads[1].wait()
    for i in range(8):
        part = jnp.zeros((128, 128), F32)
        for j in range(FEAT // 128):
            v = raw[y, i * 128:(i + 1) * 128, j * 128:(j + 1) * 128].astype(F32)
            part = part + v * v
        msg_r[t, i:i + 1, :] = jnp.sum(part.T, axis=0, keepdims=True)

    msg_b[mine] = wait_all(msg_a, t, a_s, a_r, peers_a)
    b_pushes = send_all(msg_b, mine, b_s, b_r, peers_b)
    own_pair(0)

    @pl.when(holds_prior)
    def _():
        prior_push.start()
        prior_here.start()

    sums = wait_all(msg_b, mine, b_s, b_r, peers_b)
    overall = jnp.broadcast_to(jnp.sum(sums, keepdims=True), (8, 128))
    clip_ref[...] = jnp.minimum(1.0, clip_rms * math.sqrt(D * QKV) / (jnp.sqrt(overall) + 1e-06))

    for load in loads[2:]:
        load.wait()
    za_pushes, ya_pushes, hx_pushes, zg_pushes, zf_pushes, sib_pushes, ps_pushes = {}, {}, {}, {}, {}, {}, {}

    def update(c):
        cols = slice(c * 128, (c + 1) * 128)

        def step(i, carry):
            rows = pl.ds(pl.multiple_of(i * 64, 64), 64)
            updated, _, _ = adam(
                mas[rows, cols], mom[rows, cols], sec[rows, cols], gra[rows, cols].astype(F32), clip_ref[0:1, :]
            )
            z_out[c, i // 4, pl.ds(pl.multiple_of(i % 4 * 64, 64), 64), :] = updated.astype(BF16)
            return carry

        lax.fori_loop(0, FEAT // 64, step, 0)
        for d in range(1, 4):
            za_pushes[c, d] = push(
                z_out.at[c, d], z_in.at[c, d], za_s.at[c, d - 1], za_r.at[c, d - 1], (g, (z + d) % 4 * 2 + h, t)
            )
            za_pushes[c, d].start()
        z_in[c, 0] = z_out[c, 0]

    def deal(c):
        for d in range(1, 4):
            za_pushes[c, d].wait_recv()
        for d in range(1, 4):
            other = (y + d) % 4
            ya_pushes[c, d] = push(
                z_in.at[c, (z + 4 - other) % 4], y_in.at[c, y], ya_s.at[c, d - 1], ya_r.at[c, d - 1],
                (g, f, l * 4 + other),
            )
            ya_pushes[c, d].start()
        y_in[c, y] = z_in[c, quarter]

    here = pl.ds(pl.multiple_of(h * 128, 128), 128)
    there = pl.ds(pl.multiple_of((1 - h) * 128, 128), 128)

    def part_of(c, q, cols):
        return w.at[c, :, g, q, :, cols]

    def cross(c, slot, q):
        block = part_of(c, q, here)
        hx_pushes[c, slot] = push(block, block, hx_s.at[c, slot], hx_r.at[c, slot], at_h)
        hx_pushes[c, slot].start()

    def mix(c):
        for d in range(1, 4):
            block = y_in.at[c, (y + 4 - d) % 4]
            push(block, block, ya_s.at[c, d - 1], ya_r.at[c, d - 1], (g, f, l * 4 + (y + d) % 4)).wait_recv()
        for block in range(4):
            policy = y_in[c, block].astype(F32)
            prior = pri[block, :, c * 128:(c + 1) * 128].astype(F32)
            w[c, block, g, quarter, :, here] = (mix_share * policy + (1.0 - mix_share) * prior).astype(BF16)
        cross(c, 0, quarter)

    def along_z(c, part):
        block = part_of(c, quarter, (here, there)[part])
        for way, where in ((0, at_z_up), (1, at_z_down)):
            zg_pushes[c, part, way] = push(block, block, zg_s.at[c, part, way], zg_r.at[c, part, way], where)
            zg_pushes[c, part, way].start()

    def share(c, slot, q):
        block = w.at[c, :, g, q]
        sib_pushes[c, slot] = push(block, block, sib_s.at[c, slot], sib_r.at[c, slot], at_core)
        sib_pushes[c, slot].start()

    def across(c, slot, q):
        came = part_of(c, q, there)
        push(came, came, hx_s.at[c, slot], hx_r.at[c, slot], at_h).wait_recv()

    def onward(c):
        ways = ((0, quarter_down, at_z_up), (1, quarter_up, at_z_down))
        for part in range(2):
            for way, q, where in ways:
                block = part_of(c, q, (here, there)[part])
                push(block, block, zg_s.at[c, part, way], zg_r.at[c, part, way], where).wait_recv()
                if part == way:
                    zf_pushes[c, way] = push(block, block, zf_s.at[c, way], zf_r.at[c, way], where)
                    zf_pushes[c, way].start()
        for way, q, where in ways:
            share(c, 1 + way, q)

    quarters = (quarter, quarter_down, quarter_up, quarter_far)

    def shared(c):
        for slot, q in enumerate(quarters):
            block = w.at[c, :, 1 - g, q]
            push(block, block, sib_s.at[c, slot], sib_r.at[c, slot], at_core).wait_recv()

    def half_of(c, q, way):
        return w.at[c, :, g, q, pl.ds(way * 128, 128), here]

    def onward_alone(c):
        for way, q, where in ((0, quarter_down, at_z_up), (1, quarter_up, at_z_down)):
            block = part_of(c, q, here)
            push(block, block, zg_s.at[c, 0, way], zg_r.at[c, 0, way], where).wait_recv()
            block = half_of(c, q, way)
            zf_pushes[c, way] = push(block, block, zf_s.at[c, way], zf_r.at[c, way], where)
            zf_pushes[c, way].start()
            cross(c, 1 + way, q)

    def far_alone(c):
        for way, where in ((0, at_z_up), (1, at_z_down)):
            block = half_of(c, quarter_far, way)
            push(block, block, zf_s.at[c, way], zf_r.at[c, way], where).wait_recv()
        cross(c, 3, quarter_far)

    def complete_alone(c):
        for slot, q in enumerate(quarters):
            across(c, slot, q)
            share(c, slot, q)
        shared(c)

    def complete(c):
        for way, where in ((0, at_z_up), (1, at_z_down)):
            block = part_of(c, quarter_far, (here, there)[way])
            push(block, block, zf_s.at[c, way], zf_r.at[c, way], where).wait_recv()
        share(c, 3, quarter_far)
        shared(c)

    def multiply(j, c):
        rows = pl.ds(*GROUPS[j])

        def half(panel):
            return jnp.dot(
                normed[rows, :], w[c, :, panel].reshape(4 * FEAT, 256), preferred_element_type=F32
            )

        ps_out[c, rows, :] = half(1 - l).astype(SUM_TYPE)
        ps_pushes[j, c] = push(
            ps_out.at[c, rows, :], ps_in.at[c, rows, :], ps_s.at[c, j], ps_r.at[c, j], at_x
        )
        ps_pushes[j, c].start()
        own[c, rows, :] = half(l)

    def finish(j, c):
        ps_pushes[j, c].wait_recv()
        start, count = GROUPS[j]

        def step(i, carry):
            at = pl.ds(pl.multiple_of(start + i * 64, 64), 64)
            pair = (own[c, at, :] + ps_in[c, at, :].astype(F32)) * D ** (-0.5)
            for head, values in ((c, pair[:, 0:128]), (3 + c, pair[:, 128:256])):
                if head < 5:
                    turned = jnp.concatenate([values[:, 64:], values[:, :64]], axis=1)
                    values = values * table_ref[0, at, :] + turned * table_ref[1, at, :]
                qkv[head, at, :] = values.astype(BF16)
            return carry

        lax.fori_loop(0, count // 64, step, 0)

    def key_range(j):
        return max(0, j - 2) * 256, (j + 1) * 256

    def mask(j):
        low, high = key_range(j)
        segments = seg_ref[0:1, :].astype(F32)
        column = jnp.concatenate(
            [
                jnp.broadcast_to(segments[:, s:s + 128], (128, 128)).T
                for s in range(j * 256, high, 128)
            ],
            axis=0,
        )
        same = jnp.concatenate([column] * ((high - low) // 128), axis=1) == segments[:, low:high]
        at_query = lax.broadcasted_iota(jnp.int32, (256, high - low), 0) + j * 256
        at_key = lax.broadcasted_iota(jnp.int32, (256, high - low), 1) + low
        bias[j, :, 0:high - low] = jnp.where(same & (at_query >= at_key), 0.0, -jnp.inf)

    def attend(j, head):
        low, high = key_range(j)
        scores = lax.dot_general(
            qkv[head, j * 256:high, :], qkv[QPK, low:high, :],
            (((1,), (1,)), ((), ())), preferred_element_type=F32,
        ) * HD ** (-0.5) + bias[j, :, 0:high - low]
        weights = jnp.exp(scores - jnp.max(scores, axis=1, keepdims=True))
        weights = (weights / jnp.sum(weights, axis=1, keepdims=True)).astype(BF16)
        out_ref[j * 256:high, head * HD:(head + 1) * HD] = jnp.dot(
            weights, qkv[QPK + 1, low:high, :], preferred_element_type=F32
        ).astype(BF16)

    first, second, third = ORDER

    def row_scales():
        inverse = lax.rsqrt(wait_all(msg_r, t, r_s, r_r, peers_a) / D + 1e-05)
        for i in range(8):
            inv[i * 128:(i + 1) * 128, :] = jnp.broadcast_to(inverse[i:i + 1, :], (128, 128)).T

    def prior_ready():
        @pl.when(holds_prior)
        def _():
            prior_here.wait()

        @pl.when(jnp.logical_not(holds_prior))
        def _():
            prior_push.wait_recv()

    for c in ORDER:
        update(c)
    r_pushes = send_all(msg_r, t, r_s, r_r, peers_a)
    deal(first)
    deal(second)
    prior_ready()
    mix(first)
    along_z(first, 0)
    deal(third)
    own_pair(1)
    mix(second)
    across(first, 0, quarter)
    along_z(first, 1)
    share(first, 0, quarter)
    along_z(second, 0)
    mix(third)
    forward_pair(0)
    own_pair(2)
    row_scales()
    for j in range(5):
        normalize(y, j)
    onward(first)
    across(third, 0, quarter)
    share(third, 0, quarter)
    onward_alone(second)
    along_z(third, 0)
    along_z(third, 1)
    forward_pair(1)
    for j in range(4):
        mask(j)
    ready_pair(0)
    far_alone(second)
    complete(first)
    multiply(0, first)
    forward_pair(2)
    own_pair(3)
    own_pair(4)
    ready_pair(1)
    multiply(1, first)
    onward(third)
    complete_alone(second)
    multiply(0, second)
    multiply(1, second)
    ready_pair(2)
    multiply(2, first)
    multiply(2, second)
    forward_pair(3)
    complete(third)
    for j in range(3):
        multiply(j, third)
    forward_pair(4)
    finish(0, first)
    finish(1, first)
    finish(0, second)
    attend(0, 1)
    attend(0, 2)
    finish(1, second)
    attend(1, 1)
    attend(1, 2)
    ready_pair(3)
    for c in ORDER:
        multiply(3, c)
    finish(2, first)
    finish(2, second)
    attend(2, 1)
    attend(2, 2)
    ready_pair(4)
    for c in ORDER:
        multiply(4, c)
    for j in range(3):
        finish(j, third)
        attend(j, 0)
        attend(j, 3)
    for c in ORDER:
        finish(3, c)
    finish(4, first)
    finish(4, second)
    attend(3, 1)
    attend(3, 2)
    finish(4, third)
    attend(3, 0)
    attend(3, 3)

    for copy in tok_pushes + a_pushes + b_pushes + r_pushes:
        copy.wait_send()
    for copies in (za_pushes, ya_pushes, hx_pushes, zg_pushes, zf_pushes, sib_pushes, ps_pushes):
        for copy in copies.values():
            copy.wait_send()

    @pl.when(holds_prior)
    def _():
        prior_push.wait_send()


def project(master, moment, second, gradient, prior, tokens, gain, tables, segments):
    dma = pltpu.SemaphoreType.DMA
    vmem = pl.BlockSpec(memory_space=pltpu.VMEM)
    hbm = pl.BlockSpec(memory_space=pl.ANY)
    return pl.pallas_call(
        project_kernel,
        out_shape=(
            jax.ShapeDtypeStruct((TOK, QPK * HD), BF16),
            jax.ShapeDtypeStruct((8, 128), F32),
        ),
        in_specs=[hbm] * 6 + [vmem] * 3,
        out_specs=(vmem, vmem),
        scratch_shapes=[
            pltpu.VMEM((4, TOK, FEAT), BF16),
            pltpu.VMEM((TOK, 4 * FEAT), BF16),
            pltpu.VMEM((3, 4, 2, 4, 256, 256), BF16),
            pltpu.VMEM((FEAT, COLS), F32),
            pltpu.VMEM((FEAT, COLS), F32),
            pltpu.VMEM((FEAT, COLS), F32),
            pltpu.VMEM((FEAT, COLS), BF16),
            pltpu.VMEM((TOK, 128), F32),
            pltpu.VMEM((8, 8, 128), F32),
            pltpu.VMEM((16, 8, 128), F32),
            pltpu.VMEM((8, 8, 128), F32),
            pltpu.VMEM((3, 4, 256, 128), BF16),
            pltpu.VMEM((3, 4, 256, 128), BF16),
            pltpu.VMEM((3, 4, 256, 128), BF16),
            pltpu.VMEM((4, 256, COLS), BF16),
            pltpu.VMEM((3, TOK, 256), F32),
            pltpu.VMEM((3, TOK, 256), SUM_TYPE),
            pltpu.VMEM((3, TOK, 256), SUM_TYPE),
            pltpu.VMEM((QPK + 2, TOK, HD), BF16),
            pltpu.VMEM((4, 256, 768), F32),
            dma((6,)),
            dma((2, 10)), dma((2, 10)), dma((2, 5)), dma((2, 5)),
            dma((7,)), dma((7,)), dma((15,)), dma((15,)), dma((7,)), dma((7,)),
            dma, dma,
            dma((3, 3)), dma((3, 3)), dma((3, 3)), dma((3, 3)), dma((3, 4)), dma((3, 4)),
            dma((3, 2, 2)), dma((3, 2, 2)), dma((3, 2)), dma((3, 2)),
            dma((3, 4)), dma((3, 4)), dma((3, 5)), dma((3, 5)),
        ],
        compiler_params=pltpu.CompilerParams(
            collective_id=0, has_side_effects=True, vmem_limit_bytes=54 * 1024 * 1024
        ),
        cost_estimate=pl.CostEstimate(
            flops=2 * TOK * D * 768, bytes_accessed=24 * 1024 * 1024, transcendentals=0
        ),
    )(master, moment, second, gradient, prior.reshape(8, 4, 256, 768), tokens, gain, tables, segments)


BLOCK = 256


def outputs_kernel(
    clip_ref, master_ref, moment_ref, second_ref, grad_ref, attended_ref,
    new_master_ref, new_moment_ref, new_second_ref, out_ref,
):
    def step(i, carry):
        rows = pl.ds(pl.multiple_of(i * 32, 32), 32)
        clip = jnp.concatenate([clip_ref[0:1, :]] * 3, axis=1)
        new_master, new_moment, new_second = adam(
            master_ref[rows, :], moment_ref[rows, :], second_ref[rows, :], grad_ref[rows, :].astype(F32), clip
        )
        new_master_ref[rows, :] = new_master
        new_moment_ref[rows, :] = new_moment
        new_second_ref[rows, :] = new_second
        return carry

    lax.fori_loop(0, BLOCK // 32, step, 0)
    out_ref[...] = attended_ref[...]


def outputs(clip, master, moment, second, gradient, attended):
    rows = pl.BlockSpec((BLOCK, COLS), lambda i: (i, 0))
    wide = pl.BlockSpec((BLOCK, QPK * HD), lambda i: (i, 0))
    return pl.pallas_call(
        outputs_kernel,
        grid=(TOK // BLOCK,),
        out_shape=(
            jax.ShapeDtypeStruct((FEAT, COLS), F32),
            jax.ShapeDtypeStruct((FEAT, COLS), F32),
            jax.ShapeDtypeStruct((FEAT, COLS), F32),
            jax.ShapeDtypeStruct((TOK, QPK * HD), BF16),
        ),
        in_specs=[pl.BlockSpec((8, 128), lambda i: (0, 0)), rows, rows, rows, rows, wide],
        out_specs=(rows, rows, rows, wide),
        compiler_params=pltpu.CompilerParams(vmem_limit_bytes=24 * 1024 * 1024),
    )(clip, master, moment, second, gradient, attended)


def shards(master, moment, second, gradient, prior_weights, tokens, norm_gain, segment_ids):
    attended, clip = project(
        master, moment, second, gradient, prior_weights, tokens[0], norm_gain.reshape(8, 1, FEAT),
        jnp.asarray(rotary_tables()), segment_ids,
    )
    new_master, new_moment, new_second, attended = outputs(
        clip, master, moment, second, gradient, attended
    )
    return (new_master, new_moment, new_second, attended[None])


def solution(mesh):
    in_specs = (
        P("tensor", ("group", "fsdp")),
        P("tensor", ("group", "fsdp")),
        P("tensor", ("group", "fsdp")),
        P("tensor", ("group", "fsdp")),
        P(None, "tensor"),
        P(("group", "fsdp"), None, "tensor"),
        P(),
        P(("group", "fsdp"), None),
    )
    out_specs = (
        P("tensor", ("group", "fsdp")),
        P("tensor", ("group", "fsdp")),
        P("tensor", ("group", "fsdp")),
        P(("group", "fsdp"), None, "tensor"),
    )
    return jax.shard_map(shards, mesh=mesh, in_specs=in_specs, out_specs=out_specs, check_vma=False)
```

```python
import functools
import math

import jax
import jax.numpy as jnp
import numpy as np
from jax import lax
from jax.experimental import pallas as pl
from jax.experimental.pallas import tpu as pltpu
from jax.sharding import PartitionSpec as P

D = 8192
HD = 128
QPK = 4
QKV = 6144

learn_rate = 0.01
decay_rate = 0.1
clip_rms = 0.25
first_fix = 1.0 - math.exp(200.0 * math.log(0.9))
second_fix = 1.0 - math.exp(200.0 * math.log(0.95))
mix_share = 0.6

MESH = pl.DeviceIdType.MESH
F32 = jnp.float32
BF16 = jnp.bfloat16
SUM_TYPE = BF16
TOK = 1024
FEAT = 1024
COLS = 384
GROUPS = ((0, 256), (256, 256), (512, 256), (768, 128), (896, 128))
ORDER = (2, 1, 0)


def rotary_tables():
    places = np.arange(TOK).astype(np.float32)
    lanes = np.arange(HD // 2).astype(np.float32)
    frequencies = np.power(500000.0, -(lanes * np.float32(2.0) / np.float32(HD)).astype(np.float64))
    angles = places[:, None] * frequencies.astype(np.float32)[None, :]
    cosine = np.cos(angles.astype(np.float64)).astype(np.float32)
    sine = np.sin(angles.astype(np.float64)).astype(np.float32)
    return np.stack(
        [np.concatenate([cosine, cosine], 1), np.concatenate([-sine, sine], 1)]
    ).astype(np.float32)


def adam(master, moment, second, grad, clip):
    clipped = clip * grad
    new_moment = 0.9 * moment + 0.1 * clipped
    new_second = 0.95 * second + 0.05 * clipped * clipped
    update = (
        new_moment / first_fix / (jnp.sqrt(new_second / second_fix) + 1e-08) + decay_rate * master
    )
    return master - learn_rate * update, new_moment, new_second


def push(src, dst, send, recv, where):
    return pltpu.make_async_remote_copy(
        src_ref=src, dst_ref=dst, send_sem=send, recv_sem=recv, device_id=where, device_id_type=MESH
    )


def project_kernel(
    master_ref, moment_ref, second_ref, grad_ref, prior_ref, tok_ref, table_ref, gain_ref, seg_ref,
    out_ref, clip_ref,
    raw, normed, w, mas, mom, sec, gra, inv, msg_a, msg_b, msg_r, z_out, z_in, y_in, pri, own, ps_out, ps_in, qkv, bias, table,
    load_sem, tok_s, tok_r, fwd_s, fwd_r, a_s, a_r, b_s, b_r, r_s, r_r, pri_s, pri_r,
    za_s, za_r, ya_s, ya_r, hx_s, hx_r, zg_s, zg_r, zf_s, zf_r, sib_s, sib_r, ps_s, ps_r,
):
    g = lax.axis_index("group")
    f = lax.axis_index("fsdp")
    t = lax.axis_index("tensor")
    z, h = f // 2, f % 2
    l, y = t // 4, t % 4
    y_up, y_down, y_far = (y + 1) % 4, (y + 3) % 4, (y + 2) % 4
    z_up, z_down, z_far = (z + 1) % 4, (z + 3) % 4, (z + 2) % 4
    at_y_up, at_y_down = (g, f, l * 4 + y_up), (g, f, l * 4 + y_down)
    at_z_up, at_z_down = (g, z_up * 2 + h, t), (g, z_down * 2 + h, t)
    at_x = (g, f, (1 - l) * 4 + y)
    at_h = (g, z * 2 + (1 - h), t)
    at_core = (1 - g, f, t)
    mine = g * 8 + f
    quarter = (z + 4 - y) % 4
    quarter_up, quarter_down, quarter_far = (quarter + 1) % 4, (quarter + 3) % 4, (quarter + 2) % 4

    loads = [
        pltpu.make_async_copy(grad_ref, gra, load_sem.at[0]),
        pltpu.make_async_copy(tok_ref, raw.at[y], load_sem.at[1]),
        pltpu.make_async_copy(master_ref, mas, load_sem.at[2]),
        pltpu.make_async_copy(moment_ref, mom, load_sem.at[3]),
        pltpu.make_async_copy(second_ref, sec, load_sem.at[4]),
        pltpu.make_async_copy(table_ref, table, load_sem.at[6]),
    ]
    for load in loads:
        load.start()
    prior_cols = pl.ds(pl.multiple_of(h * COLS, 128), COLS)
    prior_here = pltpu.make_async_copy(
        prior_ref.at[pl.ds(l * 4, 4), quarter, :, prior_cols], pri, load_sem.at[5]
    )
    prior_push = push(
        prior_ref.at[pl.ds((1 - l) * 4, 4), quarter, :, prior_cols], pri, pri_s, pri_r, at_x
    )
    holds_prior = g == l

    peers_a = [(g, f, (t + d) % 8) for d in range(1, 8)]
    places_b = [(mine + d) % 16 for d in range(1, 16)]
    peers_b = [(place // 8, place % 8, t) for place in places_b]

    barrier = pltpu.get_barrier_semaphore()
    for peer in peers_a + peers_b:
        pl.semaphore_signal(barrier, inc=1, device_id=peer, device_id_type=MESH)

    loads[0].wait()

    def grad_sum(i, total):
        v = gra[pl.ds(pl.multiple_of(i * 64, 64), 64), :].astype(F32)
        return total + jnp.sum((v * v).reshape(8, 8, COLS), axis=0)

    total = lax.fori_loop(0, FEAT // 64, grad_sum, jnp.zeros((8, COLS), F32))
    msg_a[t] = total[:, 0:128] + total[:, 128:256] + total[:, 256:384]
    pl.semaphore_wait(barrier, 22)

    def send_all(msg, slot, send, recv, peers):
        copies = [push(msg.at[slot], msg.at[slot], send.at[d], recv.at[d], peer) for d, peer in enumerate(peers)]
        for copy in copies:
            copy.start()
        return copies

    def wait_all(msg, slot, send, recv, peers):
        count = len(peers) + 1
        for d, peer in enumerate(peers):
            source = (slot + count - 1 - d) % count
            push(msg.at[source], msg.at[source], send.at[d], recv.at[d], peer).wait_recv()
        sums = msg[0]
        for s in range(1, count):
            sums = sums + msg[s]
        return sums

    a_pushes = send_all(msg_a, t, a_s, a_r, peers_a)

    tok_pushes = []

    def tok_rows(piece):
        start, count = GROUPS[piece // 2]
        return pl.ds(start + piece % 2 * (count // 2), count // 2)

    def own_pair(j):
        for piece in (2 * j, 2 * j + 1):
            for way, where in ((0, at_y_up), (1, at_y_down)):
                copy = push(
                    tok_ref.at[tok_rows(piece), :], raw.at[y, tok_rows(piece), :],
                    tok_s.at[way, piece], tok_r.at[way, piece], where,
                )
                copy.start()
                tok_pushes.append(copy)

    def forward_pair(j):
        for way, source, where in ((0, y_down, at_y_up), (1, y_up, at_y_down)):
            piece = 2 * j + way
            block = raw.at[source, tok_rows(piece), :]
            push(block, block, tok_s.at[way, piece], tok_r.at[way, piece], where).wait_recv()
            copy = push(block, block, fwd_s.at[way, j], fwd_r.at[way, j], where)
            copy.start()
            tok_pushes.append(copy)

    def normalize(block, j):
        gain = gain_ref[l * 4 + block]
        cols = pl.ds(pl.multiple_of(block * FEAT, FEAT), FEAT)
        start, count = GROUPS[j]

        def step(i, carry):
            rows = pl.ds(pl.multiple_of(start + i * 32, 32), 32)
            scale = jnp.concatenate([inv[rows, :]] * (FEAT // 128), axis=1)
            normed[rows, cols] = (raw[block, rows, :].astype(F32) * scale * gain).astype(BF16)
            return carry

        lax.fori_loop(0, count // 32, step, 0)

    def ready_pair(j):
        for way, source, where in ((0, y_down, at_y_up), (1, y_up, at_y_down)):
            piece = 2 * j + 1 - way
            block = raw.at[source, tok_rows(piece), :]
            push(block, block, tok_s.at[way, piece], tok_r.at[way, piece], where).wait_recv()
        normalize(y_down, j)
        normalize(y_up, j)
        for way, where in ((0, at_y_up), (1, at_y_down)):
            block = raw.at[y_far, tok_rows(2 * j + way), :]
            push(block, block, fwd_s.at[way, j], fwd_r.at[way, j], where).wait_recv()
        normalize(y_far, j)

    loads[1].wait()
    for i in range(8):
        part = jnp.zeros((128, 128), F32)
        for j in range(FEAT // 128):
            v = raw[y, i * 128:(i + 1) * 128, j * 128:(j + 1) * 128].astype(F32)
            part = part + v * v
        msg_r[t, i:i + 1, :] = jnp.sum(part.T, axis=0, keepdims=True)

    msg_b[mine] = wait_all(msg_a, t, a_s, a_r, peers_a)
    b_pushes = send_all(msg_b, mine, b_s, b_r, peers_b)
    own_pair(0)

    @pl.when(holds_prior)
    def _():
        prior_push.start()
        prior_here.start()

    sums = wait_all(msg_b, mine, b_s, b_r, peers_b)
    overall = jnp.broadcast_to(jnp.sum(sums, keepdims=True), (8, 128))
    clip_ref[...] = jnp.minimum(1.0, clip_rms * math.sqrt(D * QKV) / (jnp.sqrt(overall) + 1e-06))

    for load in loads[2:]:
        load.wait()
    za_pushes, ya_pushes, hx_pushes, zg_pushes, zf_pushes, sib_pushes, ps_pushes = {}, {}, {}, {}, {}, {}, {}

    def update(c):
        cols = slice(c * 128, (c + 1) * 128)

        def step(i, carry):
            rows = pl.ds(pl.multiple_of(i * 64, 64), 64)
            updated, _, _ = adam(
                mas[rows, cols], mom[rows, cols], sec[rows, cols], gra[rows, cols].astype(F32), clip_ref[0:1, :]
            )
            z_out[c, i // 4, pl.ds(pl.multiple_of(i % 4 * 64, 64), 64), :] = updated.astype(BF16)
            return carry

        lax.fori_loop(0, FEAT // 64, step, 0)
        for d in range(1, 4):
            za_pushes[c, d] = push(
                z_out.at[c, d], z_in.at[c, d], za_s.at[c, d - 1], za_r.at[c, d - 1], (g, (z + d) % 4 * 2 + h, t)
            )
            za_pushes[c, d].start()
        z_in[c, 0] = z_out[c, 0]

    def deal(c):
        for d in range(1, 4):
            za_pushes[c, d].wait_recv()
        for d in range(1, 4):
            other = (y + d) % 4
            ya_pushes[c, d] = push(
                z_in.at[c, (z + 4 - other) % 4], y_in.at[c, y], ya_s.at[c, d - 1], ya_r.at[c, d - 1],
                (g, f, l * 4 + other),
            )
            ya_pushes[c, d].start()
        y_in[c, y] = z_in[c, quarter]

    here = pl.ds(pl.multiple_of(h * 128, 128), 128)
    there = pl.ds(pl.multiple_of((1 - h) * 128, 128), 128)

    def part_of(c, q, cols):
        return w.at[c, :, g, q, :, cols]

    def cross(c, slot, q):
        block = part_of(c, q, here)
        hx_pushes[c, slot] = push(block, block, hx_s.at[c, slot], hx_r.at[c, slot], at_h)
        hx_pushes[c, slot].start()

    def mix(c):
        for d in range(1, 4):
            block = y_in.at[c, (y + 4 - d) % 4]
            push(block, block, ya_s.at[c, d - 1], ya_r.at[c, d - 1], (g, f, l * 4 + (y + d) % 4)).wait_recv()
        for block in range(4):
            policy = y_in[c, block].astype(F32)
            prior = pri[block, :, c * 128:(c + 1) * 128].astype(F32)
            w[c, block, g, quarter, :, here] = (mix_share * policy + (1.0 - mix_share) * prior).astype(BF16)
        cross(c, 0, quarter)

    def along_z(c, part):
        block = part_of(c, quarter, (here, there)[part])
        for way, where in ((0, at_z_up), (1, at_z_down)):
            zg_pushes[c, part, way] = push(block, block, zg_s.at[c, part, way], zg_r.at[c, part, way], where)
            zg_pushes[c, part, way].start()

    def share(c, slot, q):
        block = w.at[c, :, g, q]
        sib_pushes[c, slot] = push(block, block, sib_s.at[c, slot], sib_r.at[c, slot], at_core)
        sib_pushes[c, slot].start()

    def across(c, slot, q):
        came = part_of(c, q, there)
        push(came, came, hx_s.at[c, slot], hx_r.at[c, slot], at_h).wait_recv()

    def onward(c):
        ways = ((0, quarter_down, at_z_up), (1, quarter_up, at_z_down))
        for part in range(2):
            for way, q, where in ways:
                block = part_of(c, q, (here, there)[part])
                push(block, block, zg_s.at[c, part, way], zg_r.at[c, part, way], where).wait_recv()
                if part == way:
                    zf_pushes[c, way] = push(block, block, zf_s.at[c, way], zf_r.at[c, way], where)
                    zf_pushes[c, way].start()
        for way, q, where in ways:
            share(c, 1 + way, q)

    quarters = (quarter, quarter_down, quarter_up, quarter_far)

    def shared(c):
        for slot, q in enumerate(quarters):
            block = w.at[c, :, 1 - g, q]
            push(block, block, sib_s.at[c, slot], sib_r.at[c, slot], at_core).wait_recv()

    def half_of(c, q, way):
        return w.at[c, :, g, q, pl.ds(way * 128, 128), here]

    def onward_alone(c):
        for way, q, where in ((0, quarter_down, at_z_up), (1, quarter_up, at_z_down)):
            block = part_of(c, q, here)
            push(block, block, zg_s.at[c, 0, way], zg_r.at[c, 0, way], where).wait_recv()
            block = half_of(c, q, way)
            zf_pushes[c, way] = push(block, block, zf_s.at[c, way], zf_r.at[c, way], where)
            zf_pushes[c, way].start()
            cross(c, 1 + way, q)

    def far_alone(c):
        for way, where in ((0, at_z_up), (1, at_z_down)):
            block = half_of(c, quarter_far, way)
            push(block, block, zf_s.at[c, way], zf_r.at[c, way], where).wait_recv()
        cross(c, 3, quarter_far)

    def complete_alone(c):
        for slot, q in enumerate(quarters):
            across(c, slot, q)
            share(c, slot, q)
        shared(c)

    def complete(c):
        for way, where in ((0, at_z_up), (1, at_z_down)):
            block = part_of(c, quarter_far, (here, there)[way])
            push(block, block, zf_s.at[c, way], zf_r.at[c, way], where).wait_recv()
        share(c, 3, quarter_far)
        shared(c)

    def multiply(j, c):
        rows = pl.ds(*GROUPS[j])

        def half(panel):
            return jnp.dot(
                normed[rows, :], w[c, :, panel].reshape(4 * FEAT, 256), preferred_element_type=F32
            )

        ps_out[c, rows, :] = half(1 - l).astype(SUM_TYPE)
        ps_pushes[j, c] = push(
            ps_out.at[c, rows, :], ps_in.at[c, rows, :], ps_s.at[c, j], ps_r.at[c, j], at_x
        )
        ps_pushes[j, c].start()
        own[c, rows, :] = half(l)

    def finish(j, c):
        ps_pushes[j, c].wait_recv()
        start, count = GROUPS[j]

        def step(i, carry):
            at = pl.ds(pl.multiple_of(start + i * 64, 64), 64)
            pair = (own[c, at, :] + ps_in[c, at, :].astype(F32)) * D ** (-0.5)
            for head, values in ((c, pair[:, 0:128]), (3 + c, pair[:, 128:256])):
                if head < 5:
                    turned = jnp.concatenate([values[:, 64:], values[:, :64]], axis=1)
                    values = values * table[0, at, :] + turned * table[1, at, :]
                qkv[head, at, :] = values.astype(BF16)
            return carry

        lax.fori_loop(0, count // 64, step, 0)

    def key_range(j):
        return max(0, j - 2) * 256, (j + 1) * 256

    def mask(j):
        low, high = key_range(j)
        segments = seg_ref[0:1, :].astype(F32)
        column = jnp.concatenate(
            [
                jnp.broadcast_to(segments[:, s:s + 128], (128, 128)).T
                for s in range(j * 256, high, 128)
            ],
            axis=0,
        )
        same = jnp.concatenate([column] * ((high - low) // 128), axis=1) == segments[:, low:high]
        at_query = lax.broadcasted_iota(jnp.int32, (256, high - low), 0) + j * 256
        at_key = lax.broadcasted_iota(jnp.int32, (256, high - low), 1) + low
        bias[j, :, 0:high - low] = jnp.where(same & (at_query >= at_key), 0.0, -jnp.inf)

    def attend(j, head):
        low, high = key_range(j)
        scores = lax.dot_general(
            qkv[head, j * 256:high, :], qkv[QPK, low:high, :],
            (((1,), (1,)), ((), ())), preferred_element_type=F32,
        ) * HD ** (-0.5) + bias[j, :, 0:high - low]
        weights = jnp.exp(scores - jnp.max(scores, axis=1, keepdims=True))
        weights = (weights / jnp.sum(weights, axis=1, keepdims=True)).astype(BF16)
        out_ref[j * 256:high, head * HD:(head + 1) * HD] = jnp.dot(
            weights, qkv[QPK + 1, low:high, :], preferred_element_type=F32
        ).astype(BF16)

    first, second, third = ORDER

    def row_scales():
        inverse = lax.rsqrt(wait_all(msg_r, t, r_s, r_r, peers_a) / D + 1e-05)
        for i in range(8):
            inv[i * 128:(i + 1) * 128, :] = jnp.broadcast_to(inverse[i:i + 1, :], (128, 128)).T

    def prior_ready():
        @pl.when(holds_prior)
        def _():
            prior_here.wait()

        @pl.when(jnp.logical_not(holds_prior))
        def _():
            prior_push.wait_recv()

    for c in ORDER:
        update(c)
    r_pushes = send_all(msg_r, t, r_s, r_r, peers_a)
    deal(first)
    deal(second)
    prior_ready()
    mix(first)
    along_z(first, 0)
    deal(third)
    own_pair(1)
    mix(second)
    across(first, 0, quarter)
    along_z(first, 1)
    share(first, 0, quarter)
    along_z(second, 0)
    mix(third)
    forward_pair(0)
    own_pair(2)
    row_scales()
    for j in range(5):
        normalize(y, j)
    onward(first)
    across(third, 0, quarter)
    share(third, 0, quarter)
    onward_alone(second)
    along_z(third, 0)
    along_z(third, 1)
    forward_pair(1)
    for j in range(4):
        mask(j)
    ready_pair(0)
    far_alone(second)
    complete(first)
    multiply(0, first)
    forward_pair(2)
    own_pair(3)
    own_pair(4)
    ready_pair(1)
    multiply(1, first)
    onward(third)
    complete_alone(second)
    multiply(0, second)
    multiply(1, second)
    ready_pair(2)
    multiply(2, first)
    multiply(2, second)
    forward_pair(3)
    complete(third)
    for j in range(3):
        multiply(j, third)
    forward_pair(4)
    finish(0, first)
    finish(1, first)
    finish(0, second)
    attend(0, 1)
    attend(0, 2)
    finish(1, second)
    attend(1, 1)
    attend(1, 2)
    ready_pair(3)
    for c in ORDER:
        multiply(3, c)
    finish(2, first)
    finish(2, second)
    attend(2, 1)
    attend(2, 2)
    ready_pair(4)
    for c in ORDER:
        multiply(4, c)
    for j in range(3):
        finish(j, third)
        attend(j, 0)
        attend(j, 3)
    for c in ORDER:
        finish(3, c)
    finish(4, first)
    finish(4, second)
    attend(3, 1)
    attend(3, 2)
    finish(4, third)
    attend(3, 0)
    attend(3, 3)

    for copy in tok_pushes + a_pushes + b_pushes + r_pushes:
        copy.wait_send()
    for copies in (za_pushes, ya_pushes, hx_pushes, zg_pushes, zf_pushes, sib_pushes, ps_pushes):
        for copy in copies.values():
            copy.wait_send()

    @pl.when(holds_prior)
    def _():
        prior_push.wait_send()


def project(master, moment, second, gradient, prior, tokens, gain, tables, segments):
    dma = pltpu.SemaphoreType.DMA
    vmem = pl.BlockSpec(memory_space=pltpu.VMEM)
    hbm = pl.BlockSpec(memory_space=pl.ANY)
    return pl.pallas_call(
        project_kernel,
        out_shape=(
            jax.ShapeDtypeStruct((TOK, QPK * HD), BF16),
            jax.ShapeDtypeStruct((8, 128), F32),
        ),
        in_specs=[hbm] * 7 + [vmem] * 2,
        out_specs=(vmem, vmem),
        scratch_shapes=[
            pltpu.VMEM((4, TOK, FEAT), BF16),
            pltpu.VMEM((TOK, 4 * FEAT), BF16),
            pltpu.VMEM((3, 4, 2, 4, 256, 256), BF16),
            pltpu.VMEM((FEAT, COLS), F32),
            pltpu.VMEM((FEAT, COLS), F32),
            pltpu.VMEM((FEAT, COLS), F32),
            pltpu.VMEM((FEAT, COLS), BF16),
            pltpu.VMEM((TOK, 128), F32),
            pltpu.VMEM((8, 8, 128), F32),
            pltpu.VMEM((16, 8, 128), F32),
            pltpu.VMEM((8, 8, 128), F32),
            pltpu.VMEM((3, 4, 256, 128), BF16),
            pltpu.VMEM((3, 4, 256, 128), BF16),
            pltpu.VMEM((3, 4, 256, 128), BF16),
            pltpu.VMEM((4, 256, COLS), BF16),
            pltpu.VMEM((3, TOK, 256), F32),
            pltpu.VMEM((3, TOK, 256), SUM_TYPE),
            pltpu.VMEM((3, TOK, 256), SUM_TYPE),
            pltpu.VMEM((QPK + 2, TOK, HD), BF16),
            pltpu.VMEM((4, 256, 768), F32),
            pltpu.VMEM((2, TOK, HD), F32),
            dma((7,)),
            dma((2, 10)), dma((2, 10)), dma((2, 5)), dma((2, 5)),
            dma((7,)), dma((7,)), dma((15,)), dma((15,)), dma((7,)), dma((7,)),
            dma, dma,
            dma((3, 3)), dma((3, 3)), dma((3, 3)), dma((3, 3)), dma((3, 4)), dma((3, 4)),
            dma((3, 2, 2)), dma((3, 2, 2)), dma((3, 2)), dma((3, 2)),
            dma((3, 4)), dma((3, 4)), dma((3, 5)), dma((3, 5)),
        ],
        compiler_params=pltpu.CompilerParams(
            collective_id=0, has_side_effects=True, vmem_limit_bytes=54 * 1024 * 1024
        ),
        cost_estimate=pl.CostEstimate(
            flops=2 * TOK * D * 768, bytes_accessed=24 * 1024 * 1024, transcendentals=0
        ),
    )(master, moment, second, gradient, prior.reshape(8, 4, 256, 768), tokens, tables, gain, segments)


BLOCK = 256


def outputs_kernel(
    clip_ref, master_ref, moment_ref, second_ref, grad_ref,
    new_master_ref, new_moment_ref, new_second_ref,
):
    def step(i, carry):
        rows = pl.ds(pl.multiple_of(i * 32, 32), 32)
        clip = jnp.concatenate([clip_ref[0:1, :]] * 3, axis=1)
        new_master, new_moment, new_second = adam(
            master_ref[rows, :], moment_ref[rows, :], second_ref[rows, :], grad_ref[rows, :].astype(F32), clip
        )
        new_master_ref[rows, :] = new_master
        new_moment_ref[rows, :] = new_moment
        new_second_ref[rows, :] = new_second
        return carry

    lax.fori_loop(0, BLOCK // 32, step, 0)


def outputs(clip, master, moment, second, gradient):
    rows = pl.BlockSpec((BLOCK, COLS), lambda i: (i, 0))
    return pl.pallas_call(
        outputs_kernel,
        grid=(TOK // BLOCK,),
        out_shape=(
            jax.ShapeDtypeStruct((FEAT, COLS), F32),
            jax.ShapeDtypeStruct((FEAT, COLS), F32),
            jax.ShapeDtypeStruct((FEAT, COLS), F32),
        ),
        in_specs=[pl.BlockSpec((8, 128), lambda i: (0, 0)), rows, rows, rows, rows],
        out_specs=(rows, rows, rows),
        compiler_params=pltpu.CompilerParams(vmem_limit_bytes=24 * 1024 * 1024),
    )(clip, master, moment, second, gradient)


def shards(master, moment, second, gradient, prior_weights, tokens, norm_gain, segment_ids):
    attended, clip = project(
        master, moment, second, gradient, prior_weights, tokens[0], norm_gain.reshape(8, 1, FEAT),
        jnp.asarray(rotary_tables()), segment_ids,
    )
    new_master, new_moment, new_second = outputs(clip, master, moment, second, gradient)
    return (new_master, new_moment, new_second, attended[None])


def solution(mesh):
    in_specs = (
        P("tensor", ("group", "fsdp")),
        P("tensor", ("group", "fsdp")),
        P("tensor", ("group", "fsdp")),
        P("tensor", ("group", "fsdp")),
        P(None, "tensor"),
        P(("group", "fsdp"), None, "tensor"),
        P(),
        P(("group", "fsdp"), None),
    )
    out_specs = (
        P("tensor", ("group", "fsdp")),
        P("tensor", ("group", "fsdp")),
        P("tensor", ("group", "fsdp")),
        P(("group", "fsdp"), None, "tensor"),
    )
    return jax.shard_map(shards, mesh=mesh, in_specs=in_specs, out_specs=out_specs, check_vma=False)
```
